128 devices in a mesh: row: 16 (over z, y), col: 8 (over x, core).
Axes of the slice: x: 4, y: 4, z: 4, core: 2. Of those that a mesh axis runs over, the one named last changes fastest.
Arguments:
- matrix: bfloat16 [32768, 32768], P('row', 'col'), may hold values from -0.03125 to 0.03125
- band_mask: int32 [64, 64], P('row', 'col'), may hold values from 0 to 1, as said below
- unit_cost: float32 [32768], P('col'), may hold values from -6 to 6
- capacity: float32 [32768], P('col'), may hold values from 0.3 to 3
- demand: float32 [64, 32768], P(None, 'row'), may hold values from -6 to 6
- primal_iter: float32 [64, 32768], P(None, 'col'), may hold values from 0 to 1
- dual_iter: float32 [64, 32768], P(None, 'row'), may hold values from 0 to 1
- primal_avg: float32 [64, 32768], P(None, 'col'), may hold values from 0 to 1
- dual_avg: float32 [64, 32768], P(None, 'row'), may hold values from 0 to 1
- primal_prev: float32 [64, 32768], P(None, 'col')
- dual_prev: float32 [64, 32768], P(None, 'row')
- weight: float32 [64], replicated, may hold values from 0.5 to 2
- restart: int32 [64], replicated, may hold values from 0 to 1
- plan: int32 [64], replicated, may hold values from 0 to 3
Outputs:
- primal_next: float32 [64, 32768], P(None, 'col')
- dual_next: float32 [64, 32768], P(None, 'row')
- weight_next: float32 [64], replicated
- residual: float32 [64], P('col')
The draws below stay inside these ranges and needn't reach their ends.
Inputs may be any that keep to these rules, and one draw needn't show every extreme that they name: `band_mask`: 1 where a block of contracts may be served by a block of segments; every block of contracts has an eligible block.
All inputs are finite; a program needn't handle non-finite values.
Results may differ from the reference program's by a relative error of at most 0.00057.
Values sent between devices are 32-bit elements; how exact they have to be, the bound alone decides.
No kernel may reach another device: no remote copies, remote signals or barrier semaphores. Data moves between devices by JAX's collectives and lax.ppermute only.
A program may use at most 128 MiB of HBM per device.

```python
import math
import jax
import jax.numpy as jnp
from jax import lax

SCENARIOS = 64
SEGMENTS = 32768
BLOCK = 512
ITERS = 3
CONTRACTS = 32768


def draw_band_mask(key, part):
    key = jax.random.fold_in(key, 5)
    first_key, second_key = jax.random.split(key)
    block_rows = CONTRACTS // BLOCK
    block_cols = SEGMENTS // BLOCK
    reach = jax.random.randint(first_key, (block_rows, 1), 0, 4)
    center = (jnp.arange(block_rows, dtype=jnp.int32) * block_cols // block_rows)[:, None]
    columns = jnp.arange(block_cols, dtype=jnp.int32)[None, :]
    in_band = jnp.abs(columns - center) <= reach
    extra = jax.random.randint(second_key, (block_rows, block_cols), 0, 8) == 0
    return jnp.logical_or(in_band, extra).astype(jnp.int32)


def scaled_offsets(key, jitter, length):
    first_key, second_key = jax.random.split(key)
    scenario_scale = jnp.exp(jax.random.uniform(first_key, (SCENARIOS, 1), jnp.float32, math.log(0.05), math.log(2.0)))
    position_ramp = jnp.power(3.0, jnp.arange(length, dtype=jnp.float32) / length)[None, :]
    roughness = jnp.exp(jax.random.uniform(second_key, (SCENARIOS, length), jnp.float32, math.log(0.5), math.log(2.0)))
    return 0.5 + 0.3 * scenario_scale * position_ramp * roughness * jitter


def draw_primal_prev(key, part):
    key = jax.random.fold_in(key, 11)
    jitter_key = jax.random.fold_in(key, 1)
    jitter = jax.random.normal(jitter_key, (SCENARIOS, SEGMENTS), jnp.float32)
    return scaled_offsets(key, jitter, SEGMENTS)


def draw_dual_prev(key, part):
    key = jax.random.fold_in(key, 23)
    jitter_key = jax.random.fold_in(key, 1)
    jitter = jax.random.normal(jitter_key, (SCENARIOS, CONTRACTS), jnp.float32)
    return scaled_offsets(key, jitter, CONTRACTS)


def plant(drawn, own_key, low, high):
    place = [jax.random.randint(jax.random.fold_in(own_key, axis), (), 0, length) for axis, length in enumerate(drawn.shape)]
    widest = drawn.shape.index(max(drawn.shape))
    next_to = place[:widest] + [(place[widest] + 1) % drawn.shape[widest]] + place[widest + 1:]
    return drawn.at[tuple(place)].set(low).at[tuple(next_to)].set(high)


def levels(key, extent, pieces, least, largest):
    gain, own = 1.0, jax.random.fold_in(key, 6)
    for axis_at, blocks in pieces:
        heights = jnp.exp(jax.random.uniform(jax.random.fold_in(own, axis_at), (blocks,), jnp.float32, least / len(pieces), largest / len(pieces)))
        gain = gain * jnp.repeat(heights, extent[axis_at] // blocks).reshape([-1 if axis == axis_at else 1 for axis in range(len(extent))])
    return gain


def gaussian(key, shape, deviation, bound, pieces=(), kind=jnp.bfloat16):
    factor_of = levels(key, shape, pieces, -0.22, 0.18) if pieces else 1.0
    entries = jax.random.normal(key, shape, jnp.float32) * deviation * factor_of
    return jnp.minimum(jnp.maximum(entries, -bound), bound).astype(kind)


def setup_inputs(seed: int = 0) -> dict:
    key_list = jax.random.split(jax.random.key(seed), 15)
    return {
        "matrix": gaussian(key_list[0], (CONTRACTS, SEGMENTS), SEGMENTS ** -0.5, 0.03125, ((0, 16), (1, 8))),
        "band_mask": draw_band_mask(jax.random.fold_in(key_list[14], 71), 0),
        "unit_cost": gaussian(key_list[2], (SEGMENTS,), 1.0, 6.0, ((0, 8),), jnp.float32),
        "capacity": jnp.clip(jnp.exp(math.log(3.0) - 2.3025851 * jax.random.uniform(key_list[3], (SEGMENTS,), jnp.float32) ** levels(key_list[3], (SEGMENTS,), ((0, 8),), -0.2, 0.2)), 0.3, 3.0),
        "demand": gaussian(key_list[4], (SCENARIOS, CONTRACTS), 1.0, 6.0, ((1, 16),), jnp.float32),
        "primal_iter": jnp.clip(1.0 * jax.random.uniform(key_list[5], (SCENARIOS, SEGMENTS), jnp.float32) ** levels(key_list[5], (SCENARIOS, SEGMENTS), ((1, 8),), -0.2, 0.2), 0.0, 1.0),
        "dual_iter": jnp.clip(1.0 * jax.random.uniform(key_list[6], (SCENARIOS, CONTRACTS), jnp.float32) ** levels(key_list[6], (SCENARIOS, CONTRACTS), ((1, 16),), -0.2, 0.2), 0.0, 1.0),
        "primal_avg": jnp.clip(1.0 * jax.random.uniform(key_list[7], (SCENARIOS, SEGMENTS), jnp.float32) ** levels(key_list[7], (SCENARIOS, SEGMENTS), ((1, 8),), -0.2, 0.2), 0.0, 1.0),
        "dual_avg": jnp.clip(1.0 * jax.random.uniform(key_list[8], (SCENARIOS, CONTRACTS), jnp.float32) ** levels(key_list[8], (SCENARIOS, CONTRACTS), ((1, 16),), -0.2, 0.2), 0.0, 1.0),
        "primal_prev": draw_primal_prev(jax.random.fold_in(key_list[14], 71), 0),
        "dual_prev": draw_dual_prev(jax.random.fold_in(key_list[14], 71), 0),
        "weight": jnp.clip(jnp.exp(jax.random.uniform(key_list[11], (SCENARIOS,), jnp.float32, math.log(0.5), math.log(2.0))), 0.5, 2.0),
        "restart": plant(jax.random.randint(key_list[12], (SCENARIOS,), 0, 2), jax.random.fold_in(key_list[12], 1), 0, 1).astype(jnp.int32),
        "plan": plant(jax.random.randint(key_list[13], (SCENARIOS,), 0, 4), jax.random.fold_in(key_list[13], 1), 0, 3).astype(jnp.int32),
    }


epsilon = 1e-06

def mask_block(block, mask_row):
    columns = jnp.repeat(mask_row, BLOCK).astype(block.dtype)
    return block * columns[None, :]

def apply_matrix(vector, matrix, band_mask):
    block_rows = band_mask.shape[0]
    blocks = matrix.reshape(block_rows, BLOCK, matrix.shape[1])
    rounded = vector.astype(jnp.bfloat16)

    def one_block(pair):
        block, mask_row = pair
        return jnp.dot(rounded, mask_block(block, mask_row).T, preferred_element_type=jnp.float32)
    images = lax.map(one_block, (blocks, band_mask))
    return jnp.transpose(images, (1, 0, 2)).reshape(vector.shape[0], matrix.shape[0])

def apply_transpose(vector, matrix, band_mask):
    block_rows = band_mask.shape[0]
    blocks = matrix.reshape(block_rows, BLOCK, matrix.shape[1])
    rounded = vector.astype(jnp.bfloat16).reshape(vector.shape[0], block_rows, BLOCK)
    rounded = jnp.transpose(rounded, (1, 0, 2))

    def add_block(total, triple):
        block, mask_row, piece = triple
        return (total + jnp.dot(piece, mask_block(block, mask_row), preferred_element_type=jnp.float32), None)
    start_total = jnp.zeros((vector.shape[0], matrix.shape[1]), jnp.float32)
    total, unused = lax.scan(add_block, start_total, (blocks, band_mask, rounded))
    return total

def reference(matrix, band_mask, unit_cost, capacity, demand, primal_iter, dual_iter, primal_avg, dual_avg, primal_prev, dual_prev, weight, restart, plan):
    restarted = restart == 1
    primal_gap = lax.optimization_barrier(jnp.sum(jnp.square(primal_avg - primal_prev), axis=1))
    dual_gap = lax.optimization_barrier(jnp.sum(jnp.square(dual_avg - dual_prev), axis=1))
    weight_next = jnp.where(restarted, jnp.sqrt(weight * jnp.sqrt((dual_gap + epsilon) / (primal_gap + epsilon))), weight)
    step_size = 0.4 * jnp.power(0.75, plan.astype(jnp.float32))
    primal_size = (step_size / weight_next)[:, None]
    dual_size = (step_size * weight_next)[:, None]
    primal_now = jnp.where(restarted[:, None], primal_avg, primal_iter)
    dual_now = jnp.where(restarted[:, None], dual_avg, dual_iter)
    image = apply_matrix(primal_now, matrix, band_mask)
    for iteration in range(ITERS):
        gradient = unit_cost[None, :] - apply_transpose(dual_now, matrix, band_mask)
        primal_new = jnp.minimum(jnp.maximum(primal_now - primal_size * gradient, 0.0), capacity[None, :])
        image_new = apply_matrix(primal_new, matrix, band_mask)
        dual_now = jnp.maximum(dual_now + dual_size * (demand - 2.0 * image_new + image), 0.0)
        primal_now = primal_new
        image = image_new
    residual = jnp.sqrt(lax.optimization_barrier(jnp.mean(jnp.square(jnp.maximum(demand - image, 0.0)), axis=1)) + epsilon)
    return (primal_now, dual_now, weight_next, residual)
```

```python
import jax
import jax.numpy as jnp
from jax import lax
from jax.experimental import pallas as pl
from jax.experimental.pallas import tpu as pltpu
from jax.sharding import PartitionSpec as P

BLOCK = 512
PIECE = 256
ITERS = 3
LANES = 128
TAIL = PIECE + LANES
MIB = 2**20

epsilon = 1e-06

ROWS_BY_COLS = (((1,), (0,)), ((), ()))
ROWS_BY_ROWS = (((1,), (1,)), ((), ()))
VMEM = pl.BlockSpec(memory_space=pltpu.VMEM)
SMEM = pl.BlockSpec(memory_space=pltpu.SMEM)


def f32(*shape):
    return jax.ShapeDtypeStruct(shape, jnp.float32)


def launch(body, name, out_shape, args, smem=0, scratch=(), limit=4, flops=10**6, bytes_accessed=10**6):
    outs = jax.tree.map(lambda unused: VMEM, out_shape)
    return pl.pallas_call(
        body,
        name=name,
        out_shape=out_shape,
        in_specs=[SMEM] * smem + [VMEM] * (len(args) - smem),
        out_specs=outs,
        scratch_shapes=list(scratch),
        compiler_params=pltpu.CompilerParams(vmem_limit_bytes=limit * MIB),
        cost_estimate=pl.CostEstimate(flops=flops, bytes_accessed=bytes_accessed, transcendentals=0),
    )(*args)


def tile(matrix, i, j):
    rows = pl.ds(pl.multiple_of(i * BLOCK, BLOCK), BLOCK)
    cols = pl.ds(pl.multiple_of(j * BLOCK, BLOCK), BLOCK)
    return matrix[rows, cols]


def forward_blocks(mask, place, matrix, mine, other, rounded, acc):
    block_rows, block_cols = mask.shape

    @pl.loop(0, block_rows)
    def _(i):
        acc[...] = jnp.zeros_like(acc)

        @pl.loop(0, block_cols)
        def _(j):
            @pl.when(mask[i, j] != 0)
            def _():
                acc[...] += lax.dot_general(
                    rounded[j], tile(matrix, i, j), ROWS_BY_ROWS, preferred_element_type=jnp.float32
                )

        low = acc[:, :PIECE]
        high = acc[:, PIECE:]
        slot = lax.rem(i - place[0] + block_rows, block_rows)
        first = place[1] == 0
        mine[slot, :, :PIECE] = jnp.where(first, low, high)
        other[slot, :, :PIECE] = jnp.where(first, high, low)


def backward_blocks(mask, matrix, out, rounded, acc):
    block_rows, block_cols = mask.shape
    scenarios = acc.shape[0]

    @pl.loop(0, block_cols)
    def _(j):
        acc[...] = jnp.zeros_like(acc)

        @pl.loop(0, block_rows)
        def _(i):
            @pl.when(mask[i, j] != 0)
            def _():
                acc[...] += lax.dot_general(
                    rounded[i], tile(matrix, i, j), ROWS_BY_COLS, preferred_element_type=jnp.float32
                )

        out[2 * j, :scenarios] = acc[:, :PIECE]
        out[2 * j + 1, :scenarios] = acc[:, PIECE:]


def first_forward(mask, place, restart, avg, now, prev, matrix, mine, other, rounded, acc):
    restarted = restart[...] == 1
    gap = jnp.zeros((avg.shape[0], 1), jnp.float32)
    for j in range(mask.shape[1]):
        cols = pl.ds(j * BLOCK, BLOCK)
        rounded[j] = jnp.where(restarted, avg[:, cols], now[:, cols]).astype(jnp.bfloat16)
        gap += jnp.sum(jnp.square(avg[:, cols] - prev[:, cols]), axis=1, keepdims=True)
    forward_blocks(mask, place, matrix, mine, other, rounded, acc)
    for slot in range(mask.shape[0]):
        mine[slot, :, PIECE:] = jnp.broadcast_to(gap, (avg.shape[0], LANES))
        other[slot, :, PIECE:] = jnp.broadcast_to(gap, (avg.shape[0], LANES))


def later_forward(mask, place, pieces, matrix, mine, other, rounded, acc):
    for j in range(mask.shape[1]):
        rounded[j, :, :PIECE] = pieces[2 * j].astype(jnp.bfloat16)
        rounded[j, :, PIECE:] = pieces[2 * j + 1].astype(jnp.bfloat16)
    forward_blocks(mask, place, matrix, mine, other, rounded, acc)


def on_diagonal(rows):
    shape = (rows, LANES)
    return lax.broadcasted_iota(jnp.int32, shape, 0) == lax.broadcasted_iota(jnp.int32, shape, 1)


def first_backward(mask, restart, avg, now, prev, matrix, out, rounded, acc):
    scenarios = avg.shape[0]
    restarted = restart[...] == 1
    gap = jnp.zeros((scenarios, 1), jnp.float32)
    for i in range(mask.shape[0]):
        cols = pl.ds(i * BLOCK, BLOCK)
        rounded[i] = jnp.where(restarted, avg[:, cols], now[:, cols]).astype(jnp.bfloat16)
        gap += jnp.sum(jnp.square(avg[:, cols] - prev[:, cols]), axis=1, keepdims=True)
    backward_blocks(mask, matrix, out, rounded, acc)
    spread = jnp.where(on_diagonal(scenarios), jnp.broadcast_to(gap, (scenarios, LANES)), 0.0)
    row = jnp.broadcast_to(jnp.sum(spread, axis=0, keepdims=True), (8, LANES))
    for piece in range(out.shape[0]):
        out[piece, scenarios:, :LANES] = row
        out[piece, scenarios:, LANES:] = jnp.zeros((8, PIECE - LANES), jnp.float32)


def later_backward(mask, place, own, swapped, matrix, out, rounded, acc):
    block_rows = mask.shape[0]
    first = place[1] == 0

    @pl.loop(0, block_rows)
    def _(i):
        slot = lax.rem(i - place[0] + block_rows, block_rows)
        a = own[slot, :, :PIECE]
        b = swapped[slot, :, :PIECE]
        rounded[i, :, :PIECE] = jnp.where(first, a, b).astype(jnp.bfloat16)
        rounded[i, :, PIECE:] = jnp.where(first, b, a).astype(jnp.bfloat16)

    backward_blocks(mask, matrix, out, rounded, acc)


def add_pair(mine, received, *slots):
    for k, slot in enumerate(slots):
        slot[...] = mine[k] + received[k]


def step_primal(total, primal, cost, cap, size):
    return jnp.minimum(jnp.maximum(primal - size * (cost - total), 0.0), cap)


def spread_out(value, out):
    for piece in range(out.shape[0]):
        out[piece] = value


def first_primal(parts, near, left, across, right, weight, restart, step, primal, cost, cap, out, sizes):
    scenarios = primal.shape[0]
    total = parts[0]
    for piece in range(1, parts.shape[0]):
        total += parts[piece]
    spread = jnp.where(on_diagonal(scenarios), total[scenarios : scenarios + 1, :LANES], 0.0)
    dual_gap = jnp.sum(spread, axis=1, keepdims=True)
    gaps = near[:, PIECE:] + left[:, PIECE:] + across[:, PIECE:] + right[:, PIECE:]
    primal_gap = gaps[:, :1]
    ratio = jnp.sqrt((dual_gap + epsilon) / (primal_gap + epsilon))
    weight_next = jnp.where(restart[...] == 1, jnp.sqrt(weight[...] * ratio), weight[...])
    primal_size = step[...] / weight_next
    sizes[0] = jnp.broadcast_to(weight_next, sizes.shape[1:])
    sizes[1] = jnp.broadcast_to(primal_size, sizes.shape[1:])
    sizes[2] = jnp.broadcast_to(step[...] * weight_next, sizes.shape[1:])
    spread_out(step_primal(total[:scenarios], primal[...], cost[...], cap[...], primal_size), out)


def later_primal(parts, pieces, cost, cap, sizes, out):
    total = parts[0]
    for piece in range(1, parts.shape[0]):
        total += parts[piece]
    spread_out(step_primal(total, pieces[0], cost[...], cap[...], sizes[1, :, :1]), out)


def step_dual(near, left, across, right, image, dual, demand, sizes, image_next, dual_next):
    image_new = near[...] + left[...] + across[...] + right[...]
    moved = demand[...] - 2.0 * image_new + image[:, :PIECE]
    dual_new = jnp.maximum(dual[...] + sizes[2, :, :1] * moved, 0.0)
    image_next[...] = image_new
    dual_next[:, :PIECE] = dual_new
    if dual_next.shape[1] > PIECE:
        short = jnp.sum(jnp.square(jnp.maximum(demand[...] - image_new, 0.0)), axis=1, keepdims=True)
        dual_next[:, PIECE:] = jnp.broadcast_to(short, (short.shape[0], LANES))


def finish(place, own, swapped, dual_out, short_out):
    block_rows = own.shape[0]
    first = place[1] == 0
    short = jnp.zeros((own.shape[1], LANES), jnp.float32)
    for slot in range(block_rows):
        i = lax.rem(place[0] + slot, block_rows)
        a = own[slot, :, :PIECE]
        b = swapped[slot, :, :PIECE]
        dual_out[:, pl.ds(pl.multiple_of(i * BLOCK, BLOCK), PIECE)] = jnp.where(first, a, b)
        dual_out[:, pl.ds(pl.multiple_of(i * BLOCK + PIECE, PIECE), PIECE)] = jnp.where(first, b, a)
        short += own[slot, :, PIECE:] + swapped[slot, :, PIECE:]
    share = short_out.shape[1]
    start = (2 * place[0] + place[1]) * share
    scratch = short_out
    for piece in range(short_out.shape[0]):
        scratch[piece] = jnp.zeros((share, LANES), jnp.float32)
    for k in range(own.shape[1] // share):
        @pl.when(start == k * share)
        def _():
            for piece in range(short_out.shape[0]):
                scratch[piece] = short[k * share : (k + 1) * share]


def shards(
    matrix,
    band_mask,
    unit_cost,
    capacity,
    demand,
    primal_iter,
    dual_iter,
    primal_avg,
    dual_avg,
    primal_prev,
    dual_prev,
    weight,
    restart,
    plan,
):
    scenarios, segments = primal_iter.shape
    contracts = dual_iter.shape[1]
    block_rows, block_cols = band_mask.shape
    row_size = lax.axis_size("row")
    col_size = lax.axis_size("col")
    chips = col_size // 2
    row = lax.axis_index("row")
    col = lax.axis_index("col")
    place = jnp.stack([col // 2, col % 2]).astype(jnp.int32)
    row_first = row * PIECE
    col_first = col * PIECE
    restart_col = restart[:, None]
    weight_col = weight[:, None]
    step_col = 0.4 * jnp.power(0.75, plan.astype(jnp.float32))[:, None]

    def swap_cores(value):
        return lax.ppermute(value, "col", [(k, k ^ 1) for k in range(col_size)])

    def along_x(value, distance):
        pairs = [(k, (k + 2 * distance) % col_size) for k in range(col_size)]
        return lax.ppermute(value, "col", pairs)

    def exchange(value):
        return lax.all_to_all(value, "row", 0, 0, tiled=True)

    forward_scratch = [
        pltpu.VMEM((block_cols, scenarios, BLOCK), jnp.bfloat16),
        pltpu.VMEM((scenarios, BLOCK), jnp.float32),
    ]
    backward_scratch = [
        pltpu.VMEM((block_rows, scenarios, BLOCK), jnp.bfloat16),
        pltpu.VMEM((scenarios, BLOCK), jnp.float32),
    ]
    product_cost = dict(limit=24, flops=8 * 10**8, bytes_accessed=10**7)

    def sum_cols(mine, other):
        width = mine.shape[2]
        received = swap_cores(other)
        slots = launch(
            add_pair, "add_pair", (f32(scenarios, width),) * chips, (mine, received), limit=6
        )
        return (
            slots[0],
            along_x(slots[1], 1),
            along_x(slots[2], 2),
            along_x(slots[3], 3),
        )

    def gather_cols(value):
        own = jnp.stack([value, along_x(value, 3), along_x(value, 2), along_x(value, 1)])
        return own, swap_cores(own)

    first_out = f32(chips, scenarios, TAIL)
    mine, other = launch(
        first_forward,
        "first_forward",
        (first_out, first_out),
        (band_mask, place, restart_col, primal_avg, primal_iter, primal_prev, matrix),
        smem=2,
        scratch=forward_scratch,
        **product_cost,
    )
    parts = launch(
        first_backward,
        "first_backward",
        f32(row_size, scenarios + 8, PIECE),
        (band_mask, restart_col, dual_avg, dual_iter, dual_prev, matrix),
        smem=1,
        scratch=backward_scratch,
        **product_cost,
    )
    near, left, across, right = sum_cols(mine, other)
    parts = exchange(parts)

    def slice_start(avg, now, start):
        cut = lambda value: lax.dynamic_slice_in_dim(value, start, PIECE, 1)
        return jnp.where(restart_col == 1, cut(avg), cut(now))

    primal_slice = slice_start(primal_avg, primal_iter, row_first)
    dual = slice_start(dual_avg, dual_iter, col_first)
    cost_slice = lax.dynamic_slice_in_dim(unit_cost, row_first, PIECE, 0)[None, :]
    cap_slice = lax.dynamic_slice_in_dim(capacity, row_first, PIECE, 0)[None, :]
    demand_slice = lax.dynamic_slice_in_dim(demand, col_first, PIECE, 1)

    pieces_shape = f32(row_size, scenarios, PIECE)
    pieces, sizes = launch(
        first_primal,
        "first_primal",
        (pieces_shape, f32(3, scenarios, LANES)),
        (
            parts,
            near,
            left,
            across,
            right,
            weight_col,
            restart_col,
            step_col,
            primal_slice,
            cost_slice,
            cap_slice,
        ),
        limit=8,
    )
    image = near + left + across + right
    for iteration in range(ITERS):
        if iteration > 0:
            parts = launch(
                later_backward,
                "later_backward",
                pieces_shape,
                (band_mask, place, own, swapped, matrix),
                smem=2,
                scratch=backward_scratch,
                **product_cost,
            )
            parts = exchange(parts)
            pieces = launch(
                later_primal,
                "later_primal",
                pieces_shape,
                (parts, pieces, cost_slice, cap_slice, sizes),
                limit=8,
            )
        gathered = exchange(pieces)
        slots_shape = f32(chips, scenarios, PIECE)
        mine, other = launch(
            later_forward,
            "later_forward",
            (slots_shape, slots_shape),
            (band_mask, place, gathered, matrix),
            smem=2,
            scratch=forward_scratch,
            **product_cost,
        )
        near, left, across, right = sum_cols(mine, other)
        width = TAIL if iteration == ITERS - 1 else PIECE
        image, dual = launch(
            step_dual,
            "step_dual",
            (f32(scenarios, PIECE), f32(scenarios, width)),
            (near, left, across, right, image, dual, demand_slice, sizes),
        )
        own, swapped = gather_cols(dual)

    share = scenarios // col_size
    dual_next, short = launch(
        finish,
        "finish",
        (f32(scenarios, contracts), f32(row_size, share, LANES)),
        (place, own, swapped),
        smem=1,
        limit=6,
    )
    short = jnp.sum(exchange(short), axis=0)[:, 0]
    residual = jnp.sqrt(short / (contracts * row_size) + epsilon)
    primal_next = jnp.transpose(gathered, (1, 0, 2)).reshape(scenarios, segments)
    return (primal_next, dual_next, sizes[0, :, 0], residual)


def solution(mesh):
    in_specs = (
        P("row", "col"),
        P("row", "col"),
        P("col"),
        P("col"),
        P(None, "row"),
        P(None, "col"),
        P(None, "row"),
        P(None, "col"),
        P(None, "row"),
        P(None, "col"),
        P(None, "row"),
        P(),
        P(),
        P(),
    )
    out_specs = (P(None, "col"), P(None, "row"), P(), P("col"))
    return jax.shard_map(shards, mesh=mesh, in_specs=in_specs, out_specs=out_specs, check_vma=False)
```

```python
import jax
import jax.numpy as jnp
from jax import lax
from jax.experimental import pallas as pl
from jax.experimental.pallas import tpu as pltpu
from jax.sharding import PartitionSpec as P

BLOCK = 512
PIECE = 256
ITERS = 3
LANES = 128
MIB = 2**20

epsilon = 1e-06

ROWS_BY_COLS = (((1,), (0,)), ((), ()))
ROWS_BY_ROWS = (((1,), (1,)), ((), ()))
VMEM = pl.BlockSpec(memory_space=pltpu.VMEM)
SMEM = pl.BlockSpec(memory_space=pltpu.SMEM)
HBM = pl.BlockSpec(memory_space=pltpu.HBM)


def f32(*shape):
    return jax.ShapeDtypeStruct(shape, jnp.float32)


def bf16(*shape):
    return jax.ShapeDtypeStruct(shape, jnp.bfloat16)


def launch(body, name, out_shape, args, smem=0, hbm=0, scratch=(), limit=4, flops=10**6, bytes_accessed=10**6):
    outs = jax.tree.map(lambda unused: VMEM, out_shape)
    return pl.pallas_call(
        body,
        name=name,
        out_shape=out_shape,
        in_specs=[SMEM] * smem + [HBM] * hbm + [VMEM] * (len(args) - smem - hbm),
        out_specs=outs,
        scratch_shapes=list(scratch),
        compiler_params=pltpu.CompilerParams(vmem_limit_bytes=limit * MIB),
        cost_estimate=pl.CostEstimate(flops=flops, bytes_accessed=bytes_accessed, transcendentals=0),
    )(*args)


def span(index, size):
    return pl.ds(pl.multiple_of(index * size, size), size)


def column(row):
    n = row.shape[1]
    shape = (n, n)
    diagonal = lax.broadcasted_iota(jnp.int32, shape, 0) == lax.broadcasted_iota(jnp.int32, shape, 1)
    return jnp.sum(jnp.where(diagonal, jnp.broadcast_to(row, shape), 0), axis=1, keepdims=True)


def as_row(col):
    shape = (col.shape[0], LANES)
    diagonal = lax.broadcasted_iota(jnp.int32, shape, 0) == lax.broadcasted_iota(jnp.int32, shape, 1)
    row = jnp.sum(jnp.where(diagonal, jnp.broadcast_to(col, shape), 0.0), axis=0, keepdims=True)
    return jnp.broadcast_to(row, (8, LANES))


def fetch_blocks(mask, matrix, held, sems, by_rows):
    block_rows, block_cols = mask.shape

    def copy(i, j):
        part = (span(i, BLOCK), span(j, BLOCK))
        return pltpu.make_async_copy(matrix.at[part], held.at[part], sems.at[i, j])

    outer, inner = (block_rows, block_cols) if by_rows else (block_cols, block_rows)

    @pl.loop(0, outer)
    def _(a):
        @pl.loop(0, inner)
        def _(b):
            i, j = (a, b) if by_rows else (b, a)

            @pl.when(mask[i, j] != 0)
            def _():
                copy(i, j).start()

    return lambda i, j: copy(i, j).wait()


def nothing(i, j):
    return None


def packed_mask(bits, shape):
    word = bits[0, 0]
    return lambda i, j: jnp.bitwise_and(lax.shift_right_logical(word, i * shape[1] + j), 1)


def sum_blocks(eligible, count, multiply, acc, picked):
    found = jnp.int32(0)
    for k in range(count):
        picked[found] = k
        found = found + eligible(k)
    picked[found] = count
    acc[...] = jnp.zeros_like(acc)

    @pl.loop(0, (found + 1) // 2)
    def _(pair):
        one = picked[2 * pair]
        two = picked[2 * pair + 1]
        acc[...] += multiply(one, one) + multiply(two, jnp.where(two == count, one, two))


def blocks_of(matrix):
    return matrix.shape[0] // BLOCK, matrix.shape[1] // BLOCK


def backward_blocks(mask, direct, rounded, held, acc, picked, ready):
    block_rows, block_cols = blocks_of(held)
    scenarios = acc.shape[0]
    rounded[block_rows] = jnp.zeros(rounded.shape[1:], jnp.bfloat16)

    @pl.loop(0, block_cols)
    def _(j):
        if ready is not nothing:
            @pl.loop(0, block_rows)
            def _(i):
                @pl.when(mask(i, j) != 0)
                def _():
                    ready(i, j)

        def multiply(vector, i):
            return lax.dot_general(
                rounded[vector], held[span(i, BLOCK), span(j, BLOCK)], ROWS_BY_COLS, preferred_element_type=jnp.float32
            )

        sum_blocks(lambda i: mask(i, j), block_rows, multiply, acc, picked)
        for q in range(BLOCK // PIECE):
            direct[(BLOCK // PIECE) * j + q, :scenarios] = acc[:, q * PIECE : (q + 1) * PIECE]


def first_backward(
    mask, matrix, avg, now, prev, restart, direct, rounded, acc, picked, held, vectors, sems, few
):
    copies = [
        pltpu.make_async_copy(source, vectors.at[k], few.at[k]) for k, source in enumerate((avg, now, prev))
    ]
    for each in copies:
        each.start()
    ready = fetch_blocks(mask, matrix, held, sems, False)
    for each in copies:
        each.wait()
    scenarios = avg.shape[0]
    restarted = column(restart[...]) == 1
    gap = jnp.zeros((scenarios, 1), jnp.float32)
    for i in range(mask.shape[0]):
        cols = slice(i * BLOCK, (i + 1) * BLOCK)
        rounded[i] = jnp.where(restarted, vectors[0, :, cols], vectors[1, :, cols]).astype(jnp.bfloat16)
        gap += jnp.sum(jnp.square(vectors[0, :, cols] - vectors[2, :, cols]), axis=1, keepdims=True)
    backward_blocks(lambda i, j: mask[i, j], direct, rounded, held, acc, picked, ready)
    row = as_row(gap)
    for piece in range(direct.shape[0]):
        direct[piece, scenarios:, :LANES] = row
        direct[piece, scenarios:, LANES:] = jnp.zeros_like(row)


def here():
    col = lax.axis_index("col")
    return col // 2, lax.rem(col, 2)


def later_backward(bits, matrix, own, swapped, direct, rounded, acc, picked):
    shape = blocks_of(matrix)
    block_rows = shape[0]
    chip, core = here()
    first = core == 0

    @pl.loop(0, block_rows)
    def _(i):
        slot = lax.rem(i - chip + block_rows, block_rows)
        a = own[slot]
        b = swapped[slot]
        rounded[i, :, :PIECE] = jnp.where(first, a, b).astype(jnp.bfloat16)
        rounded[i, :, PIECE:] = jnp.where(first, b, a).astype(jnp.bfloat16)

    backward_blocks(packed_mask(bits, shape), direct, rounded, matrix, acc, picked, nothing)


def place_pieces(i, value, mine, other, lanes):
    chip, core = here()
    chips = mine.shape[0]
    slot = lax.rem(i - chip + chips, chips)
    low = value[:, :PIECE]
    high = value[:, PIECE:]
    mine[slot, :, lanes] = jnp.where(core == 0, low, high)
    other[slot, :, lanes] = jnp.where(core == 0, high, low)


def forward_blocks(bits, matrix, mine, other, rounded, acc, picked):
    shape = block_rows, block_cols = blocks_of(matrix)
    mask = packed_mask(bits, shape)
    scenarios = mine.shape[1]
    rounded[block_cols] = jnp.zeros(rounded.shape[1:], jnp.bfloat16)

    @pl.loop(0, block_rows)
    def _(i):
        def multiply(vector, j):
            return lax.dot_general(
                rounded[vector], matrix[span(i, BLOCK), span(j, BLOCK)], ROWS_BY_ROWS, preferred_element_type=jnp.float32
            )

        sum_blocks(lambda j: mask(i, j), block_cols, multiply, acc, picked)
        for group in range(acc.shape[0] // scenarios):
            lanes = slice(group * PIECE, (group + 1) * PIECE)
            place_pieces(i, acc[group * scenarios : (group + 1) * scenarios], mine, other, lanes)


def round_pieces(direct, rounded):
    scenarios = direct.shape[1]
    for piece in range(direct.shape[0]):
        cols = slice(piece % 2 * PIECE, (piece % 2 + 1) * PIECE)
        rounded[piece // 2, :scenarios, cols] = direct[piece].astype(jnp.bfloat16)


def first_forward(bits, matrix, direct, start, mine, other, rounded, acc, picked):
    scenarios = start.shape[1]
    for j in range(start.shape[0]):
        rounded[j, scenarios:] = start[j]
    round_pieces(direct, rounded)
    forward_blocks(bits, matrix, mine, other, rounded, acc, picked)


def later_forward(bits, matrix, direct, mine, other, rounded, acc, picked):
    round_pieces(direct, rounded)
    forward_blocks(bits, matrix, mine, other, rounded, acc, picked)


def prepare(avg, now, prev, restart, gap, rounded):
    restarted = column(restart[...]) == 1
    total = jnp.zeros((avg.shape[0], 1), jnp.float32)
    for j in range(rounded.shape[0]):
        cols = slice(j * BLOCK, (j + 1) * BLOCK)
        rounded[j] = jnp.where(restarted, avg[:, cols], now[:, cols]).astype(jnp.bfloat16)
        total += jnp.sum(jnp.square(avg[:, cols] - prev[:, cols]), axis=1, keepdims=True)
    gap[...] = jnp.broadcast_to(total, gap.shape)


def add_pair(mine, received, *slots):
    for k, slot in enumerate(slots):
        slot[...] = mine[k] + received[k]


def sum_parts(parts):
    total = parts[0]
    for piece in range(1, parts.shape[0]):
        total += parts[piece]
    return total


def step_primal(total, primal, cost, cap, size):
    return jnp.minimum(jnp.maximum(primal - size * (cost[...] - total), 0.0), cap[...])


def spread(value, out):
    for piece in range(out.shape[0]):
        out[piece] = value


def first_primal(
    parts, near, left, across, right, weight, restart, step, primal, cost, cap, out, sizes
):
    total = sum_parts(parts)
    scenarios = primal.shape[0]
    dual_gap = column(total[scenarios : scenarios + 1, :scenarios])
    primal_gap = (near[...] + left[...] + across[...] + right[...])[:, :1]
    old = column(weight[...])
    length = column(step[...])
    ratio = jnp.sqrt((dual_gap + epsilon) / (primal_gap + epsilon))
    weight_next = jnp.where(column(restart[...]) == 1, jnp.sqrt(old * ratio), old)
    primal_size = length / weight_next
    sizes[0] = jnp.broadcast_to(weight_next, sizes.shape[1:])
    sizes[1] = jnp.broadcast_to(primal_size, sizes.shape[1:])
    sizes[2] = jnp.broadcast_to(length * weight_next, sizes.shape[1:])
    spread(step_primal(total[:scenarios], primal[...], cost, cap, primal_size), out)


def later_primal(parts, pieces, cost, cap, sizes, out):
    spread(step_primal(sum_parts(parts), pieces[0], cost, cap, sizes[1, :, :1]), out)


def move_dual(near, left, across, right, image, dual, demand, sizes, image_next, dual_next):
    total = near[...] + left[...] + across[...] + right[...]
    image_new = total[:, :PIECE]
    image_old = total[:, PIECE:] if image is None else image[...]
    moved = demand[...] - 2.0 * image_new + image_old
    dual_next[...] = jnp.maximum(dual[...] + sizes[2, :, :1] * moved, 0.0)
    if image_next is not None:
        image_next[...] = image_new
    return image_new


def later_dual(*refs):
    move_dual(*refs)


def first_dual(near, left, across, right, dual, demand, sizes, image_next, dual_next):
    move_dual(near, left, across, right, None, dual, demand, sizes, image_next, dual_next)


def last_dual(near, left, across, right, image, dual, demand, sizes, dual_next, short_out):
    image_new = move_dual(near, left, across, right, image, dual, demand, sizes, None, dual_next)
    short = jnp.sum(jnp.square(jnp.maximum(demand[...] - image_new, 0.0)), axis=1, keepdims=True)
    row = as_row(short)
    for piece in range(short_out.shape[0]):
        short_out[piece] = row


def sum_rows(parts, out):
    out[...] = sum_parts(parts)


def finish(own, swapped, dual_out):
    block_rows = own.shape[0]
    chip, core = here()
    first = core == 0
    for slot in range(block_rows):
        i = lax.rem(chip + slot, block_rows)
        a = own[slot]
        b = swapped[slot]
        dual_out[:, span(2 * i, PIECE)] = jnp.where(first, a, b)
        dual_out[:, span(2 * i + 1, PIECE)] = jnp.where(first, b, a)


def shards(
    matrix,
    band_mask,
    unit_cost,
    capacity,
    demand,
    primal_iter,
    dual_iter,
    primal_avg,
    dual_avg,
    primal_prev,
    dual_prev,
    weight,
    restart,
    plan,
):
    scenarios, segments = primal_iter.shape
    contracts = dual_iter.shape[1]
    block_rows, block_cols = band_mask.shape
    row_size = lax.axis_size("row")
    col_size = lax.axis_size("col")
    chips = col_size // 2
    row = lax.axis_index("row")
    col = lax.axis_index("col")
    blocks = block_rows * block_cols
    bits = jnp.sum(lax.shift_left(band_mask.reshape(blocks), jnp.arange(blocks, dtype=jnp.int32)))
    bits = jnp.broadcast_to(bits, (8, LANES))
    restart_row = restart[None, :]
    weight_row = weight[None, :]
    step_row = (0.4 * jnp.power(0.75, plan.astype(jnp.float32)))[None, :]

    def swap_cores(value):
        return lax.ppermute(value, "col", [(k, k ^ 1) for k in range(col_size)])

    def along_x(value, distance):
        pairs = [(k, (k + 2 * distance) % col_size) for k in range(col_size)]
        return lax.ppermute(value, "col", pairs)

    def exchange(value):
        return lax.all_to_all(value, "row", 0, 0, tiled=True)

    def send(move, slots):
        far = move(slots[2], 2)
        return (slots[0], move(slots[1], 1), far, move(slots[3], 3))

    def spread_round(move, value):
        far = move(value, 2)
        return (value, move(value, 3), far, move(value, 1))

    picked = pltpu.SMEM((block_cols + 2,), jnp.int32)
    acc = pltpu.VMEM((scenarios, BLOCK), jnp.float32)

    def forward_scratch(count):
        return [
            pltpu.VMEM((block_cols + 1, count, BLOCK), jnp.bfloat16),
            pltpu.VMEM((count, BLOCK), jnp.float32),
            picked,
        ]

    backward_scratch = [pltpu.VMEM((block_rows + 1, scenarios, BLOCK), jnp.bfloat16), acc, picked]
    product = dict(limit=20, flops=8 * 10**8, bytes_accessed=10**7)

    def gather_cols(value):
        own = jnp.stack(spread_round(along_x, value))
        return own, swap_cores(own)

    pieces_shape = f32(row_size, scenarios, PIECE)
    parts = launch(
        first_backward,
        "first_backward",
        f32(row_size, scenarios + 8, PIECE),
        (band_mask, matrix, dual_avg, dual_iter, dual_prev, restart_row),
        smem=1,
        hbm=4,
        scratch=backward_scratch
        + [
            pltpu.VMEM(matrix.shape, jnp.bfloat16),
            pltpu.VMEM((3, scenarios, contracts), jnp.float32),
            pltpu.SemaphoreType.DMA((block_rows, block_cols)),
            pltpu.SemaphoreType.DMA((3,)),
        ],
        **dict(product, limit=60),
    )
    parts, avg, now, prev = lax.optimization_barrier((parts, primal_avg, primal_iter, primal_prev))
    parts = exchange(parts)
    gap, start = launch(
        prepare,
        "prepare",
        (f32(scenarios, LANES), bf16(block_cols, scenarios, BLOCK)),
        (avg, now, prev, restart_row),
        limit=12,
    )
    gap, bits, start = lax.optimization_barrier((gap, bits, start))
    gap = gap + swap_cores(gap)
    gaps = send(along_x, (gap,) * chips)

    def slice_start(avg, now, first):
        cut = lambda value: lax.dynamic_slice_in_dim(value, first, PIECE, 1)
        return jnp.where(restart[:, None] == 1, cut(avg), cut(now))

    primal = slice_start(primal_avg, primal_iter, row * PIECE)
    cost = lax.dynamic_slice_in_dim(unit_cost, row * PIECE, PIECE, 0)[None, :]
    cap = lax.dynamic_slice_in_dim(capacity, row * PIECE, PIECE, 0)[None, :]
    dual = slice_start(dual_avg, dual_iter, col * PIECE)
    demand_slice = lax.dynamic_slice_in_dim(demand, col * PIECE, PIECE, 1)

    pieces, sizes = launch(
        first_primal,
        "first_primal",
        (pieces_shape, f32(3, scenarios, LANES)),
        (parts, *gaps, weight_row, restart_row, step_row, primal, cost, cap),
        limit=8,
        bytes_accessed=4 * 10**7,
    )
    for iteration in range(ITERS):
        if iteration > 0:
            parts = launch(
                later_backward,
                "later_backward",
                pieces_shape,
                (bits, matrix, own, swapped),
                scratch=backward_scratch,
                **product,
            )
            parts = exchange(parts)
            pieces = launch(
                later_primal, "later_primal", pieces_shape, (parts, pieces, cost, cap, sizes), limit=8
            )
        gathered = exchange(pieces)
        if iteration == 0:
            body, count, extra = first_forward, 2 * scenarios, (start,)
        else:
            body, count, extra = later_forward, scenarios, ()
        width = count // scenarios * PIECE
        slots_shape = f32(chips, scenarios, width)
        mine, other = launch(
            body,
            "forward",
            (slots_shape, slots_shape),
            (bits, matrix, gathered, *extra),
            scratch=forward_scratch(count),
            **product,
        )
        received = swap_cores(other)
        if iteration == ITERS - 1:
            primal_next = jnp.transpose(gathered, (1, 0, 2)).reshape(scenarios, segments)
            weight_next = sizes[0, :, 0]
            received, primal_next, weight_next = lax.optimization_barrier((received, primal_next, weight_next))
        slots = launch(add_pair, "add_pair", (f32(scenarios, width),) * chips, (mine, received), limit=8)
        arrived = send(along_x, slots)
        own_value = f32(scenarios, PIECE)
        if iteration == 0:
            image, dual = launch(
                first_dual, "first_dual", (own_value, own_value), (*arrived, dual, demand_slice, sizes)
            )
        elif iteration < ITERS - 1:
            image, dual = launch(
                later_dual, "later_dual", (own_value, own_value), (*arrived, image, dual, demand_slice, sizes)
            )
        else:
            dual, short = launch(
                last_dual,
                "last_dual",
                (own_value, f32(row_size, 8, LANES)),
                (*arrived, image, dual, demand_slice, sizes),
            )
            short = exchange(short)
        own, swapped = gather_cols(dual)

    dual_next = launch(finish, "finish", f32(scenarios, contracts), (own, swapped))
    short = launch(sum_rows, "sum_rows", f32(8, LANES), (short,))
    short = short + swap_cores(short)
    short = sum(send(along_x, (short,) * chips))
    share = scenarios // col_size
    short = lax.dynamic_slice_in_dim(short[0], col * share, share, 0)
    residual = jnp.sqrt(short / (contracts * row_size) + epsilon)
    return (primal_next, dual_next, weight_next, residual)


def solution(mesh):
    in_specs = (
        P("row", "col"),
        P("row", "col"),
        P("col"),
        P("col"),
        P(None, "row"),
        P(None, "col"),
        P(None, "row"),
        P(None, "col"),
        P(None, "row"),
        P(None, "col"),
        P(None, "row"),
        P(),
        P(),
        P(),
    )
    out_specs = (P(None, "col"), P(None, "row"), P(), P("col"))
    return jax.shard_map(shards, mesh=mesh, in_specs=in_specs, out_specs=out_specs, check_vma=False)
```

```python
import jax
import jax.numpy as jnp
from jax import lax
from jax.experimental import pallas as pl
from jax.experimental.pallas import tpu as pltpu
from jax.sharding import PartitionSpec as P

BLOCK = 512
PIECE = 256
ITERS = 3
LANES = 128
MIB = 2**20

epsilon = 1e-06

ROWS_BY_COLS = (((1,), (0,)), ((), ()))
ROWS_BY_ROWS = (((1,), (1,)), ((), ()))
VMEM = pl.BlockSpec(memory_space=pltpu.VMEM)
SMEM = pl.BlockSpec(memory_space=pltpu.SMEM)
HBM = pl.BlockSpec(memory_space=pltpu.HBM)


def f32(*shape):
    return jax.ShapeDtypeStruct(shape, jnp.float32)


def bf16(*shape):
    return jax.ShapeDtypeStruct(shape, jnp.bfloat16)


def launch(body, name, out_shape, args, smem=0, hbm=0, scratch=(), limit=4, flops=10**6, bytes_accessed=10**6):
    outs = jax.tree.map(lambda unused: VMEM, out_shape)
    return pl.pallas_call(
        body,
        name=name,
        out_shape=out_shape,
        in_specs=[SMEM] * smem + [HBM] * hbm + [VMEM] * (len(args) - smem - hbm),
        out_specs=outs,
        scratch_shapes=list(scratch),
        compiler_params=pltpu.CompilerParams(vmem_limit_bytes=limit * MIB),
        cost_estimate=pl.CostEstimate(flops=flops, bytes_accessed=bytes_accessed, transcendentals=0),
    )(*args)


def span(index, size):
    return pl.ds(pl.multiple_of(index * size, size), size)


def column(row):
    n = row.shape[1]
    shape = (n, n)
    diagonal = lax.broadcasted_iota(jnp.int32, shape, 0) == lax.broadcasted_iota(jnp.int32, shape, 1)
    return jnp.sum(jnp.where(diagonal, jnp.broadcast_to(row, shape), 0), axis=1, keepdims=True)


def as_row(col):
    shape = (col.shape[0], LANES)
    diagonal = lax.broadcasted_iota(jnp.int32, shape, 0) == lax.broadcasted_iota(jnp.int32, shape, 1)
    row = jnp.sum(jnp.where(diagonal, jnp.broadcast_to(col, shape), 0.0), axis=0, keepdims=True)
    return jnp.broadcast_to(row, (8, LANES))


def blocks_of(matrix):
    return matrix.shape[0] // BLOCK, matrix.shape[1] // BLOCK


def fetch_blocks(eligible, matrix, held, sems, by_rows):
    block_rows, block_cols = blocks_of(matrix)

    def copy(i, j):
        part = (span(i, BLOCK), span(j, BLOCK))
        return pltpu.make_async_copy(matrix.at[part], held.at[part], sems.at[i, j])

    outer, inner = (block_rows, block_cols) if by_rows else (block_cols, block_rows)

    @pl.loop(0, outer)
    def _(a):
        @pl.loop(0, inner)
        def _(b):
            i, j = (a, b) if by_rows else (b, a)

            @pl.when(eligible(i, j) != 0)
            def _():
                copy(i, j).start()

    return lambda i, j: copy(i, j).wait()


def nothing(i, j):
    return None


def packed_mask(bits, shape):
    word = bits[0, 0]
    return lambda i, j: jnp.bitwise_and(lax.shift_right_logical(word, i * shape[1] + j), 1)


def sum_blocks(eligible, count, multiply, ready, acc, picked):
    found = jnp.int32(0)
    for k in range(count):
        picked[found] = k
        found = found + eligible(k)
    picked[found] = count
    acc[...] = jnp.zeros_like(acc)

    @pl.loop(0, (found + 1) // 2)
    def _(pair):
        one = picked[2 * pair]
        two = picked[2 * pair + 1]
        if ready is not nothing:
            ready(one)

            @pl.when(two != count)
            def _():
                ready(two)

        acc[...] += multiply(one, one) + multiply(two, jnp.where(two == count, one, two))


def backward_blocks(mask, direct, rounded, held, acc, picked, ready):
    block_rows, block_cols = blocks_of(held)
    scenarios = acc.shape[0]
    rounded[block_rows] = jnp.zeros(rounded.shape[1:], jnp.bfloat16)

    @pl.loop(0, block_cols)
    def _(j):
        def multiply(vector, i):
            return lax.dot_general(
                rounded[vector], held[span(i, BLOCK), span(j, BLOCK)], ROWS_BY_COLS, preferred_element_type=jnp.float32
            )

        wait = nothing if ready is nothing else lambda i: ready(i, j)
        sum_blocks(lambda i: mask(i, j), block_rows, multiply, wait, acc, picked)
        for q in range(BLOCK // PIECE):
            direct[(BLOCK // PIECE) * j + q, :scenarios] = acc[:, q * PIECE : (q + 1) * PIECE]


def first_backward(
    mask, matrix, avg, now, prev, restart, direct, rounded, acc, picked, held, vectors, sems, few
):
    copies = [
        pltpu.make_async_copy(source, vectors.at[k], few.at[k]) for k, source in enumerate((avg, now, prev))
    ]
    for each in copies:
        each.start()
    eligible = lambda i, j: mask[i, j]
    ready = fetch_blocks(eligible, matrix, held, sems, False)
    for each in copies:
        each.wait()
    scenarios = avg.shape[0]
    restarted = column(restart[...]) == 1
    gap = jnp.zeros((scenarios, 1), jnp.float32)
    for i in range(mask.shape[0]):
        cols = slice(i * BLOCK, (i + 1) * BLOCK)
        rounded[i] = jnp.where(restarted, vectors[0, :, cols], vectors[1, :, cols]).astype(jnp.bfloat16)
        gap += jnp.sum(jnp.square(vectors[0, :, cols] - vectors[2, :, cols]), axis=1, keepdims=True)
    backward_blocks(eligible, direct, rounded, held, acc, picked, ready)
    row = as_row(gap)
    for piece in range(direct.shape[0]):
        direct[piece, scenarios:, :LANES] = row
        direct[piece, scenarios:, LANES:] = jnp.zeros_like(row)


def here():
    col = lax.axis_index("col")
    return col // 2, lax.rem(col, 2)


def later_backward(bits, matrix, own, swapped, direct, rounded, acc, picked):
    shape = blocks_of(matrix)
    block_rows = shape[0]
    chip, core = here()
    first = core == 0

    @pl.loop(0, block_rows)
    def _(i):
        slot = lax.rem(i - chip + block_rows, block_rows)
        a = own[slot]
        b = swapped[slot]
        rounded[i, :, :PIECE] = jnp.where(first, a, b).astype(jnp.bfloat16)
        rounded[i, :, PIECE:] = jnp.where(first, b, a).astype(jnp.bfloat16)

    backward_blocks(packed_mask(bits, shape), direct, rounded, matrix, acc, picked, nothing)


def place_pieces(i, value, mine, other, lanes):
    chip, core = here()
    chips = mine.shape[0]
    slot = lax.rem(i - chip + chips, chips)
    low = value[:, :PIECE]
    high = value[:, PIECE:]
    mine[slot, :, lanes] = jnp.where(core == 0, low, high)
    other[slot, :, lanes] = jnp.where(core == 0, high, low)


def forward_blocks(eligible, matrix, mine, other, rounded, acc, picked, ready):
    block_rows, block_cols = blocks_of(matrix)
    scenarios = mine.shape[1]
    rounded[block_cols] = jnp.zeros(rounded.shape[1:], jnp.bfloat16)

    @pl.loop(0, block_rows)
    def _(i):
        def multiply(vector, j):
            return lax.dot_general(
                rounded[vector], matrix[span(i, BLOCK), span(j, BLOCK)], ROWS_BY_ROWS, preferred_element_type=jnp.float32
            )

        wait = nothing if ready is nothing else lambda j: ready(i, j)
        sum_blocks(lambda j: eligible(i, j), block_cols, multiply, wait, acc, picked)
        for group in range(acc.shape[0] // scenarios):
            lanes = slice(group * PIECE, (group + 1) * PIECE)
            place_pieces(i, acc[group * scenarios : (group + 1) * scenarios], mine, other, lanes)


def round_pieces(direct, rounded):
    scenarios = direct.shape[1]
    for piece in range(direct.shape[0]):
        cols = slice(piece % 2 * PIECE, (piece % 2 + 1) * PIECE)
        rounded[piece // 2, :scenarios, cols] = direct[piece].astype(jnp.bfloat16)


def first_forward(matrix, bits, direct, start, mine, other, rounded, acc, picked, held, sems):
    eligible = packed_mask(bits, blocks_of(matrix))
    ready = fetch_blocks(eligible, matrix, held, sems, True)
    scenarios = start.shape[1]
    for j in range(start.shape[0]):
        rounded[j, scenarios:] = start[j]
    round_pieces(direct, rounded)
    forward_blocks(eligible, held, mine, other, rounded, acc, picked, ready)


def later_forward(bits, matrix, direct, mine, other, rounded, acc, picked):
    round_pieces(direct, rounded)
    eligible = packed_mask(bits, blocks_of(matrix))
    forward_blocks(eligible, matrix, mine, other, rounded, acc, picked, nothing)


def prepare(avg, now, prev, restart, gap, rounded):
    restarted = column(restart[...]) == 1
    total = jnp.zeros((avg.shape[0], 1), jnp.float32)
    for j in range(rounded.shape[0]):
        cols = slice(j * BLOCK, (j + 1) * BLOCK)
        rounded[j] = jnp.where(restarted, avg[:, cols], now[:, cols]).astype(jnp.bfloat16)
        total += jnp.sum(jnp.square(avg[:, cols] - prev[:, cols]), axis=1, keepdims=True)
    gap[...] = jnp.broadcast_to(total, gap.shape)


def hold(matrix, near, out):
    out[...] = near[:8, :LANES]


def add_pair(mine, received, *slots):
    for k, slot in enumerate(slots):
        slot[...] = mine[k] + received[k]


def sum_parts(parts):
    total = parts[0]
    for piece in range(1, parts.shape[0]):
        total += parts[piece]
    return total


def step_primal(total, primal, cost, cap, size):
    return jnp.minimum(jnp.maximum(primal - size * (cost[...] - total), 0.0), cap[...])


def spread(value, out):
    for piece in range(out.shape[0]):
        out[piece] = value


def first_primal(
    parts, near, left, across, right, weight, restart, step, primal, cost, cap, out, sizes
):
    total = sum_parts(parts)
    scenarios = primal.shape[0]
    dual_gap = column(total[scenarios : scenarios + 1, :scenarios])
    primal_gap = (near[...] + left[...] + across[...] + right[...])[:, :1]
    old = column(weight[...])
    length = column(step[...])
    ratio = jnp.sqrt((dual_gap + epsilon) / (primal_gap + epsilon))
    weight_next = jnp.where(column(restart[...]) == 1, jnp.sqrt(old * ratio), old)
    primal_size = length / weight_next
    sizes[0] = jnp.broadcast_to(weight_next, sizes.shape[1:])
    sizes[1] = jnp.broadcast_to(primal_size, sizes.shape[1:])
    sizes[2] = jnp.broadcast_to(length * weight_next, sizes.shape[1:])
    spread(step_primal(total[:scenarios], primal[...], cost, cap, primal_size), out)


def later_primal(parts, pieces, cost, cap, sizes, out):
    spread(step_primal(sum_parts(parts), pieces[0], cost, cap, sizes[1, :, :1]), out)


def move_dual(near, left, across, right, image, dual, demand, sizes, image_next, dual_next):
    total = near[...] + left[...] + across[...] + right[...]
    image_new = total[:, :PIECE]
    image_old = total[:, PIECE:] if image is None else image[...]
    moved = demand[...] - 2.0 * image_new + image_old
    dual_next[...] = jnp.maximum(dual[...] + sizes[2, :, :1] * moved, 0.0)
    if image_next is not None:
        image_next[...] = image_new
    return image_new


def later_dual(*refs):
    move_dual(*refs)


def first_dual(held, near, left, across, right, dual, demand, sizes, image_next, dual_next):
    move_dual(near, left, across, right, None, dual, demand, sizes, image_next, dual_next)


def last_dual(near, left, across, right, image, dual, demand, sizes, dual_next, short_out):
    image_new = move_dual(near, left, across, right, image, dual, demand, sizes, None, dual_next)
    short = jnp.sum(jnp.square(jnp.maximum(demand[...] - image_new, 0.0)), axis=1, keepdims=True)
    row = as_row(short)
    for piece in range(short_out.shape[0]):
        short_out[piece] = row


def sum_rows(parts, out):
    out[...] = sum_parts(parts)


def finish(own, swapped, dual_out):
    block_rows = own.shape[0]
    chip, core = here()
    first = core == 0
    for slot in range(block_rows):
        i = lax.rem(chip + slot, block_rows)
        a = own[slot]
        b = swapped[slot]
        dual_out[:, span(2 * i, PIECE)] = jnp.where(first, a, b)
        dual_out[:, span(2 * i + 1, PIECE)] = jnp.where(first, b, a)


def shards(
    matrix,
    band_mask,
    unit_cost,
    capacity,
    demand,
    primal_iter,
    dual_iter,
    primal_avg,
    dual_avg,
    primal_prev,
    dual_prev,
    weight,
    restart,
    plan,
):
    scenarios, segments = primal_iter.shape
    contracts = dual_iter.shape[1]
    block_rows, block_cols = band_mask.shape
    row_size = lax.axis_size("row")
    col_size = lax.axis_size("col")
    chips = col_size // 2
    row = lax.axis_index("row")
    col = lax.axis_index("col")
    blocks = block_rows * block_cols
    bits = jnp.sum(lax.shift_left(band_mask.reshape(blocks), jnp.arange(blocks, dtype=jnp.int32)))
    bits = jnp.broadcast_to(bits, (8, LANES))
    restart_row = restart[None, :]
    weight_row = weight[None, :]
    step_row = (0.4 * jnp.power(0.75, plan.astype(jnp.float32)))[None, :]

    def swap_cores(value):
        return lax.ppermute(value, "col", [(k, k ^ 1) for k in range(col_size)])

    def along_x(value, distance):
        pairs = [(k, (k + 2 * distance) % col_size) for k in range(col_size)]
        return lax.ppermute(value, "col", pairs)

    def exchange(value):
        return lax.all_to_all(value, "row", 0, 0, tiled=True)

    def send(move, slots):
        far = move(slots[2], 2)
        return (slots[0], move(slots[1], 1), far, move(slots[3], 3))

    def spread_round(move, value):
        far = move(value, 2)
        return (value, move(value, 3), far, move(value, 1))

    picked = pltpu.SMEM((block_cols + 2,), jnp.int32)
    block_sems = pltpu.SemaphoreType.DMA((block_rows, block_cols))
    acc = pltpu.VMEM((scenarios, BLOCK), jnp.float32)

    def forward_scratch(count):
        return [
            pltpu.VMEM((block_cols + 1, count, BLOCK), jnp.bfloat16),
            pltpu.VMEM((count, BLOCK), jnp.float32),
            picked,
        ]

    backward_scratch = [pltpu.VMEM((block_rows + 1, scenarios, BLOCK), jnp.bfloat16), acc, picked]
    product = dict(limit=20, flops=8 * 10**8, bytes_accessed=10**7)

    def gather_cols(value):
        own = jnp.stack(spread_round(along_x, value))
        return own, swap_cores(own)

    pieces_shape = f32(row_size, scenarios, PIECE)
    parts = launch(
        first_backward,
        "first_backward",
        f32(row_size, scenarios + 8, PIECE),
        (band_mask, matrix, dual_avg, dual_iter, dual_prev, restart_row),
        smem=1,
        hbm=4,
        scratch=backward_scratch
        + [
            pltpu.VMEM(matrix.shape, jnp.bfloat16),
            pltpu.VMEM((3, scenarios, contracts), jnp.float32),
            block_sems,
            pltpu.SemaphoreType.DMA((3,)),
        ],
        **dict(product, limit=60),
    )
    parts, avg, now, prev = lax.optimization_barrier((parts, primal_avg, primal_iter, primal_prev))
    parts = exchange(parts)
    gap, start = launch(
        prepare,
        "prepare",
        (f32(scenarios, LANES), bf16(block_cols, scenarios, BLOCK)),
        (avg, now, prev, restart_row),
        limit=12,
    )
    gap, bits, start = lax.optimization_barrier((gap, bits, start))
    gap = gap + swap_cores(gap)
    gaps = send(along_x, (gap,) * chips)

    def slice_start(avg, now, first):
        cut = lambda value: lax.dynamic_slice_in_dim(value, first, PIECE, 1)
        return jnp.where(restart[:, None] == 1, cut(avg), cut(now))

    primal = slice_start(primal_avg, primal_iter, row * PIECE)
    cost = lax.dynamic_slice_in_dim(unit_cost, row * PIECE, PIECE, 0)[None, :]
    cap = lax.dynamic_slice_in_dim(capacity, row * PIECE, PIECE, 0)[None, :]
    dual = slice_start(dual_avg, dual_iter, col * PIECE)
    demand_slice = lax.dynamic_slice_in_dim(demand, col * PIECE, PIECE, 1)

    pieces, sizes = launch(
        first_primal,
        "first_primal",
        (pieces_shape, f32(3, scenarios, LANES)),
        (parts, *gaps, weight_row, restart_row, step_row, primal, cost, cap),
        limit=8,
        bytes_accessed=4 * 10**7,
    )
    for iteration in range(ITERS):
        if iteration > 0:
            parts = launch(
                later_backward,
                "later_backward",
                pieces_shape,
                (bits, matrix, own, swapped),
                scratch=backward_scratch,
                **product,
            )
            parts = exchange(parts)
            pieces = launch(
                later_primal, "later_primal", pieces_shape, (parts, pieces, cost, cap, sizes), limit=8
            )
        gathered = exchange(pieces)
        width = 2 * PIECE if iteration == 0 else PIECE
        slots_shape = f32(chips, scenarios, width)
        if iteration == 0:
            mine, other = launch(
                first_forward,
                "first_forward",
                (slots_shape, slots_shape),
                (matrix, bits, gathered, start),
                hbm=1,
                scratch=forward_scratch(2 * scenarios) + [pltpu.VMEM(matrix.shape, jnp.bfloat16), block_sems],
                **dict(product, limit=52),
            )
        else:
            mine, other = launch(
                later_forward,
                "later_forward",
                (slots_shape, slots_shape),
                (bits, matrix, gathered),
                scratch=forward_scratch(scenarios),
                **product,
            )
        received = swap_cores(other)
        if iteration == ITERS - 1:
            primal_next = jnp.transpose(gathered, (1, 0, 2)).reshape(scenarios, segments)
            weight_next = sizes[0, :, 0]
            received, primal_next, weight_next = lax.optimization_barrier((received, primal_next, weight_next))
        slots = launch(add_pair, "add_pair", (f32(scenarios, width),) * chips, (mine, received), limit=8)
        arrived = send(along_x, slots)
        own_value = f32(scenarios, PIECE)
        if iteration == 0:
            taken = launch(hold, "hold", f32(8, LANES), (matrix, slots[0]), limit=20)
            image, dual = launch(
                first_dual,
                "first_dual",
                (own_value, own_value),
                (taken, *arrived, dual, demand_slice, sizes),
            )
        elif iteration < ITERS - 1:
            image, dual = launch(
                later_dual, "later_dual", (own_value, own_value), (*arrived, image, dual, demand_slice, sizes)
            )
        else:
            dual, short = launch(
                last_dual,
                "last_dual",
                (own_value, f32(row_size, 8, LANES)),
                (*arrived, image, dual, demand_slice, sizes),
            )
            short = exchange(short)
        own, swapped = gather_cols(dual)

    dual_next = launch(finish, "finish", f32(scenarios, contracts), (own, swapped))
    short = launch(sum_rows, "sum_rows", f32(8, LANES), (short,))
    short = short + swap_cores(short)
    short = sum(send(along_x, (short,) * chips))
    share = scenarios // col_size
    short = lax.dynamic_slice_in_dim(short[0], col * share, share, 0)
    residual = jnp.sqrt(short / (contracts * row_size) + epsilon)
    return (primal_next, dual_next, weight_next, residual)


def solution(mesh):
    in_specs = (
        P("row", "col"),
        P("row", "col"),
        P("col"),
        P("col"),
        P(None, "row"),
        P(None, "col"),
        P(None, "row"),
        P(None, "col"),
        P(None, "row"),
        P(None, "col"),
        P(None, "row"),
        P(),
        P(),
        P(),
    )
    out_specs = (P(None, "col"), P(None, "row"), P(), P("col"))
    return jax.shard_map(shards, mesh=mesh, in_specs=in_specs, out_specs=out_specs, check_vma=False)
```

```python
import jax
import jax.numpy as jnp
from jax import lax
from jax.experimental import pallas as pl
from jax.experimental.pallas import tpu as pltpu
from jax.sharding import PartitionSpec as P

BLOCK = 512
PIECE = 256
ITERS = 3
LANES = 128
MIB = 2**20

epsilon = 1e-06

ROWS_BY_COLS = (((1,), (0,)), ((), ()))
ROWS_BY_ROWS = (((1,), (1,)), ((), ()))
VMEM = pl.BlockSpec(memory_space=pltpu.VMEM)
SMEM = pl.BlockSpec(memory_space=pltpu.SMEM)
HBM = pl.BlockSpec(memory_space=pltpu.HBM)


def f32(*shape):
    return jax.ShapeDtypeStruct(shape, jnp.float32)


def bf16(*shape):
    return jax.ShapeDtypeStruct(shape, jnp.bfloat16)


def launch(body, name, out_shape, args, smem=0, hbm=0, scratch=(), limit=4, flops=10**6, bytes_accessed=10**6):
    outs = jax.tree.map(lambda unused: VMEM, out_shape)
    return pl.pallas_call(
        body,
        name=name,
        out_shape=out_shape,
        in_specs=[SMEM] * smem + [HBM] * hbm + [VMEM] * (len(args) - smem - hbm),
        out_specs=outs,
        scratch_shapes=list(scratch),
        compiler_params=pltpu.CompilerParams(vmem_limit_bytes=limit * MIB),
        cost_estimate=pl.CostEstimate(flops=flops, bytes_accessed=bytes_accessed, transcendentals=0),
    )(*args)


def span(index, size):
    return pl.ds(pl.multiple_of(index * size, size), size)


def column(row):
    n = row.shape[1]
    shape = (n, n)
    diagonal = lax.broadcasted_iota(jnp.int32, shape, 0) == lax.broadcasted_iota(jnp.int32, shape, 1)
    return jnp.sum(jnp.where(diagonal, jnp.broadcast_to(row, shape), 0), axis=1, keepdims=True)


def as_row(col):
    shape = (col.shape[0], LANES)
    diagonal = lax.broadcasted_iota(jnp.int32, shape, 0) == lax.broadcasted_iota(jnp.int32, shape, 1)
    row = jnp.sum(jnp.where(diagonal, jnp.broadcast_to(col, shape), 0.0), axis=0, keepdims=True)
    return jnp.broadcast_to(row, (8, LANES))


def blocks_of(matrix):
    return matrix.shape[0] // BLOCK, matrix.shape[1] // BLOCK


def fetch_blocks(eligible, matrix, held, sems, by_rows):
    block_rows, block_cols = blocks_of(matrix)

    def copy(i, j):
        part = (span(i, BLOCK), span(j, BLOCK))
        return pltpu.make_async_copy(matrix.at[part], held.at[part], sems.at[i, j])

    outer, inner = (block_rows, block_cols) if by_rows else (block_cols, block_rows)

    @pl.loop(0, outer)
    def _(a):
        @pl.loop(0, inner)
        def _(b):
            i, j = (a, b) if by_rows else (b, a)

            @pl.when(eligible(i, j) != 0)
            def _():
                copy(i, j).start()

    return lambda i, j: copy(i, j).wait()


def nothing(i, j):
    return None


def packed_mask(bits, shape):
    word = bits[0, 0]
    return lambda i, j: jnp.bitwise_and(lax.shift_right_logical(word, i * shape[1] + j), 1)


def sum_blocks(eligible, count, multiply, ready, acc, picked):
    found = jnp.int32(0)
    for k in range(count):
        picked[found] = k
        found = found + eligible(k)
    acc[...] = jnp.zeros_like(acc)

    def add(first, number):
        chosen = [picked[first + k] for k in range(number)]
        for k in chosen:
            ready(k)
        terms = [multiply(k) for k in chosen]
        while len(terms) > 1:
            terms = [sum(terms[k : k + 2]) for k in range(0, len(terms), 2)]
        acc[...] += terms[0]

    fours = found // 4

    @pl.loop(0, fours)
    def _(four):
        add(4 * four, 4)

    @pl.when(found - 4 * fours >= 2)
    def _():
        add(4 * fours, 2)

    @pl.when(lax.rem(found, 2) == 1)
    def _():
        add(found - 1, 1)


def backward_blocks(mask, direct, rounded, held, acc, picked, ready):
    block_rows, block_cols = blocks_of(held)
    scenarios = acc.shape[0]

    @pl.loop(0, block_cols)
    def _(j):
        def multiply(i):
            return lax.dot_general(
                rounded[i], held[span(i, BLOCK), span(j, BLOCK)], ROWS_BY_COLS, preferred_element_type=jnp.float32
            )

        sum_blocks(lambda i: mask(i, j), block_rows, multiply, lambda i: ready(i, j), acc, picked)
        for q in range(BLOCK // PIECE):
            direct[(BLOCK // PIECE) * j + q, :scenarios] = acc[:, q * PIECE : (q + 1) * PIECE]


def first_backward(
    mask, matrix, avg, now, prev, restart, direct, rounded, acc, picked, held, vectors, sems, few
):
    copies = [
        pltpu.make_async_copy(source, vectors.at[k], few.at[k]) for k, source in enumerate((avg, now, prev))
    ]
    for each in copies:
        each.start()
    eligible = lambda i, j: mask[i, j]
    ready = fetch_blocks(eligible, matrix, held, sems, False)
    for each in copies:
        each.wait()
    scenarios = avg.shape[0]
    restarted = column(restart[...]) == 1
    gap = jnp.zeros((scenarios, 1), jnp.float32)
    for i in range(mask.shape[0]):
        cols = slice(i * BLOCK, (i + 1) * BLOCK)
        rounded[i] = jnp.where(restarted, vectors[0, :, cols], vectors[1, :, cols]).astype(jnp.bfloat16)
        gap += jnp.sum(jnp.square(vectors[0, :, cols] - vectors[2, :, cols]), axis=1, keepdims=True)
    backward_blocks(eligible, direct, rounded, held, acc, picked, ready)
    row = as_row(gap)
    for piece in range(direct.shape[0]):
        direct[piece, scenarios:, :LANES] = row
        direct[piece, scenarios:, LANES:] = jnp.zeros_like(row)


def here():
    col = lax.axis_index("col")
    return col // 2, lax.rem(col, 2)


def later_backward(bits, matrix, own, swapped, direct, rounded, acc, picked):
    shape = blocks_of(matrix)
    block_rows = shape[0]
    chip, core = here()
    first = core == 0

    @pl.loop(0, block_rows)
    def _(i):
        slot = lax.rem(i - chip + block_rows, block_rows)
        a = own[slot]
        b = swapped[slot]
        rounded[i, :, :PIECE] = jnp.where(first, a, b).astype(jnp.bfloat16)
        rounded[i, :, PIECE:] = jnp.where(first, b, a).astype(jnp.bfloat16)

    backward_blocks(packed_mask(bits, shape), direct, rounded, matrix, acc, picked, nothing)


def place_pieces(i, value, mine, other, lanes):
    chip, core = here()
    chips = mine.shape[0]
    slot = lax.rem(i - chip + chips, chips)
    low = value[:, :PIECE]
    high = value[:, PIECE:]
    mine[slot, :, lanes] = jnp.where(core == 0, low, high)
    other[slot, :, lanes] = jnp.where(core == 0, high, low)


def forward_blocks(eligible, matrix, mine, other, rounded, acc, picked, ready):
    block_rows, block_cols = blocks_of(matrix)
    scenarios = mine.shape[1]

    @pl.loop(0, block_rows)
    def _(i):
        def multiply(j):
            return lax.dot_general(
                rounded[j], matrix[span(i, BLOCK), span(j, BLOCK)], ROWS_BY_ROWS, preferred_element_type=jnp.float32
            )

        sum_blocks(lambda j: eligible(i, j), block_cols, multiply, lambda j: ready(i, j), acc, picked)
        for group in range(acc.shape[0] // scenarios):
            lanes = slice(group * PIECE, (group + 1) * PIECE)
            place_pieces(i, acc[group * scenarios : (group + 1) * scenarios], mine, other, lanes)


def round_pieces(direct, rounded):
    scenarios = direct.shape[1]
    for piece in range(direct.shape[0]):
        cols = slice(piece % 2 * PIECE, (piece % 2 + 1) * PIECE)
        rounded[piece // 2, :scenarios, cols] = direct[piece].astype(jnp.bfloat16)


def first_forward(matrix, bits, direct, start, mine, other, rounded, acc, picked, held, sems):
    eligible = packed_mask(bits, blocks_of(matrix))
    ready = fetch_blocks(eligible, matrix, held, sems, True)
    scenarios = start.shape[1]
    for j in range(start.shape[0]):
        rounded[j, scenarios:] = start[j]
    round_pieces(direct, rounded)
    forward_blocks(eligible, held, mine, other, rounded, acc, picked, ready)


def later_forward(bits, matrix, direct, mine, other, rounded, acc, picked):
    round_pieces(direct, rounded)
    eligible = packed_mask(bits, blocks_of(matrix))
    forward_blocks(eligible, matrix, mine, other, rounded, acc, picked, nothing)


def prepare(avg, now, prev, restart, gap, rounded):
    restarted = column(restart[...]) == 1
    total = jnp.zeros((avg.shape[0], 1), jnp.float32)
    for j in range(rounded.shape[0]):
        cols = slice(j * BLOCK, (j + 1) * BLOCK)
        rounded[j] = jnp.where(restarted, avg[:, cols], now[:, cols]).astype(jnp.bfloat16)
        total += jnp.sum(jnp.square(avg[:, cols] - prev[:, cols]), axis=1, keepdims=True)
    gap[...] = jnp.broadcast_to(total, gap.shape)


def hold(matrix, near, out):
    out[...] = near[:8, :LANES]


def add_pair(mine, received, *slots):
    for k, slot in enumerate(slots):
        slot[...] = mine[k] + received[k]


def sum_parts(parts):
    total = parts[0]
    for piece in range(1, parts.shape[0]):
        total += parts[piece]
    return total


def step_primal(total, primal, cost, cap, size):
    return jnp.minimum(jnp.maximum(primal - size * (cost[...] - total), 0.0), cap[...])


def spread(value, out):
    for piece in range(out.shape[0]):
        out[piece] = value


def first_primal(
    parts, near, left, across, right, weight, restart, step, primal, cost, cap, out, sizes
):
    total = sum_parts(parts)
    scenarios = primal.shape[0]
    dual_gap = column(total[scenarios : scenarios + 1, :scenarios])
    primal_gap = (near[...] + left[...] + across[...] + right[...])[:, :1]
    old = column(weight[...])
    length = column(step[...])
    ratio = jnp.sqrt((dual_gap + epsilon) / (primal_gap + epsilon))
    weight_next = jnp.where(column(restart[...]) == 1, jnp.sqrt(old * ratio), old)
    primal_size = length / weight_next
    sizes[0] = jnp.broadcast_to(weight_next, sizes.shape[1:])
    sizes[1] = jnp.broadcast_to(primal_size, sizes.shape[1:])
    sizes[2] = jnp.broadcast_to(length * weight_next, sizes.shape[1:])
    spread(step_primal(total[:scenarios], primal[...], cost, cap, primal_size), out)


def later_primal(parts, pieces, cost, cap, sizes, out):
    spread(step_primal(sum_parts(parts), pieces[0], cost, cap, sizes[1, :, :1]), out)


def move_dual(near, left, across, right, image, dual, demand, sizes, image_next, dual_next):
    total = near[...] + left[...] + across[...] + right[...]
    image_new = total[:, :PIECE]
    image_old = total[:, PIECE:] if image is None else image[...]
    moved = demand[...] - 2.0 * image_new + image_old
    dual_next[...] = jnp.maximum(dual[...] + sizes[2, :, :1] * moved, 0.0)
    if image_next is not None:
        image_next[...] = image_new
    return image_new


def later_dual(*refs):
    move_dual(*refs)


def first_dual(held, near, left, across, right, dual, demand, sizes, image_next, dual_next):
    move_dual(near, left, across, right, None, dual, demand, sizes, image_next, dual_next)


def last_dual(near, left, across, right, image, dual, demand, sizes, dual_next, short_out):
    image_new = move_dual(near, left, across, right, image, dual, demand, sizes, None, dual_next)
    short = jnp.sum(jnp.square(jnp.maximum(demand[...] - image_new, 0.0)), axis=1, keepdims=True)
    row = as_row(short)
    for piece in range(short_out.shape[0]):
        short_out[piece] = row


def sum_rows(parts, out):
    out[...] = sum_parts(parts)


def finish(own, swapped, dual_out):
    block_rows = own.shape[0]
    chip, core = here()
    first = core == 0
    for slot in range(block_rows):
        i = lax.rem(chip + slot, block_rows)
        a = own[slot]
        b = swapped[slot]
        dual_out[:, span(2 * i, PIECE)] = jnp.where(first, a, b)
        dual_out[:, span(2 * i + 1, PIECE)] = jnp.where(first, b, a)


def shards(
    matrix,
    band_mask,
    unit_cost,
    capacity,
    demand,
    primal_iter,
    dual_iter,
    primal_avg,
    dual_avg,
    primal_prev,
    dual_prev,
    weight,
    restart,
    plan,
):
    scenarios, segments = primal_iter.shape
    contracts = dual_iter.shape[1]
    block_rows, block_cols = band_mask.shape
    row_size = lax.axis_size("row")
    col_size = lax.axis_size("col")
    chips = col_size // 2
    row = lax.axis_index("row")
    col = lax.axis_index("col")
    blocks = block_rows * block_cols
    bits = jnp.sum(lax.shift_left(band_mask.reshape(blocks), jnp.arange(blocks, dtype=jnp.int32)))
    bits = jnp.broadcast_to(bits, (8, LANES))
    restart_row = restart[None, :]
    weight_row = weight[None, :]
    step_row = (0.4 * jnp.power(0.75, plan.astype(jnp.float32)))[None, :]

    def swap_cores(value):
        return lax.ppermute(value, "col", [(k, k ^ 1) for k in range(col_size)])

    def along_x(value, distance):
        pairs = [(k, (k + 2 * distance) % col_size) for k in range(col_size)]
        return lax.ppermute(value, "col", pairs)

    def exchange(value):
        return lax.all_to_all(value, "row", 0, 0, tiled=True)

    def send(move, slots):
        far = move(slots[2], 2)
        return (slots[0], move(slots[1], 1), far, move(slots[3], 3))

    def spread_round(move, value):
        far = move(value, 2)
        return (value, move(value, 3), far, move(value, 1))

    picked = pltpu.SMEM((block_cols,), jnp.int32)
    block_sems = pltpu.SemaphoreType.DMA((block_rows, block_cols))
    acc = pltpu.VMEM((scenarios, BLOCK), jnp.float32)

    def forward_scratch(count):
        return [
            pltpu.VMEM((block_cols, count, BLOCK), jnp.bfloat16),
            pltpu.VMEM((count, BLOCK), jnp.float32),
            picked,
        ]

    backward_scratch = [pltpu.VMEM((block_rows, scenarios, BLOCK), jnp.bfloat16), acc, picked]
    product = dict(limit=20, flops=8 * 10**8, bytes_accessed=10**7)

    def gather_cols(value):
        own = jnp.stack(spread_round(along_x, value))
        return own, swap_cores(own)

    pieces_shape = f32(row_size, scenarios, PIECE)
    parts = launch(
        first_backward,
        "first_backward",
        f32(row_size, scenarios + 8, PIECE),
        (band_mask, matrix, dual_avg, dual_iter, dual_prev, restart_row),
        smem=1,
        hbm=4,
        scratch=backward_scratch
        + [
            pltpu.VMEM(matrix.shape, jnp.bfloat16),
            pltpu.VMEM((3, scenarios, contracts), jnp.float32),
            block_sems,
            pltpu.SemaphoreType.DMA((3,)),
        ],
        **dict(product, limit=60),
    )
    parts, avg, now, prev = lax.optimization_barrier((parts, primal_avg, primal_iter, primal_prev))
    parts = exchange(parts)
    gap, start = launch(
        prepare,
        "prepare",
        (f32(scenarios, LANES), bf16(block_cols, scenarios, BLOCK)),
        (avg, now, prev, restart_row),
        limit=12,
    )
    gap, bits, start = lax.optimization_barrier((gap, bits, start))
    gap = gap + swap_cores(gap)
    gaps = send(along_x, (gap,) * chips)

    def slice_start(avg, now, first):
        cut = lambda value: lax.dynamic_slice_in_dim(value, first, PIECE, 1)
        return jnp.where(restart[:, None] == 1, cut(avg), cut(now))

    primal = slice_start(primal_avg, primal_iter, row * PIECE)
    cost = lax.dynamic_slice_in_dim(unit_cost, row * PIECE, PIECE, 0)[None, :]
    cap = lax.dynamic_slice_in_dim(capacity, row * PIECE, PIECE, 0)[None, :]
    dual = slice_start(dual_avg, dual_iter, col * PIECE)
    demand_slice = lax.dynamic_slice_in_dim(demand, col * PIECE, PIECE, 1)

    pieces, sizes = launch(
        first_primal,
        "first_primal",
        (pieces_shape, f32(3, scenarios, LANES)),
        (parts, *gaps, weight_row, restart_row, step_row, primal, cost, cap),
        limit=8,
        bytes_accessed=4 * 10**7,
    )
    for iteration in range(ITERS):
        if iteration > 0:
            parts = launch(
                later_backward,
                "later_backward",
                pieces_shape,
                (bits, matrix, own, swapped),
                scratch=backward_scratch,
                **product,
            )
            parts = exchange(parts)
            pieces = launch(
                later_primal, "later_primal", pieces_shape, (parts, pieces, cost, cap, sizes), limit=8
            )
        gathered = exchange(pieces)
        width = 2 * PIECE if iteration == 0 else PIECE
        slots_shape = f32(chips, scenarios, width)
        if iteration == 0:
            mine, other = launch(
                first_forward,
                "first_forward",
                (slots_shape, slots_shape),
                (matrix, bits, gathered, start),
                hbm=1,
                scratch=forward_scratch(2 * scenarios) + [pltpu.VMEM(matrix.shape, jnp.bfloat16), block_sems],
                **dict(product, limit=52),
            )
        else:
            mine, other = launch(
                later_forward,
                "later_forward",
                (slots_shape, slots_shape),
                (bits, matrix, gathered),
                scratch=forward_scratch(scenarios),
                **product,
            )
        received = swap_cores(other)
        if iteration == ITERS - 1:
            primal_next = jnp.transpose(gathered, (1, 0, 2)).reshape(scenarios, segments)
            weight_next = sizes[0, :, 0]
            received, primal_next, weight_next = lax.optimization_barrier((received, primal_next, weight_next))
        slots = launch(add_pair, "add_pair", (f32(scenarios, width),) * chips, (mine, received), limit=8)
        arrived = send(along_x, slots)
        own_value = f32(scenarios, PIECE)
        if iteration == 0:
            taken = launch(hold, "hold", f32(8, LANES), (matrix, slots[0]), limit=20)
            image, dual = launch(
                first_dual,
                "first_dual",
                (own_value, own_value),
                (taken, *arrived, dual, demand_slice, sizes),
            )
        elif iteration < ITERS - 1:
            image, dual = launch(
                later_dual, "later_dual", (own_value, own_value), (*arrived, image, dual, demand_slice, sizes)
            )
        else:
            dual, short = launch(
                last_dual,
                "last_dual",
                (own_value, f32(row_size, 8, LANES)),
                (*arrived, image, dual, demand_slice, sizes),
            )
            short = exchange(short)
        own, swapped = gather_cols(dual)

    dual_next = launch(finish, "finish", f32(scenarios, contracts), (own, swapped))
    short = launch(sum_rows, "sum_rows", f32(8, LANES), (short,))
    short = short + swap_cores(short)
    short = sum(send(along_x, (short,) * chips))
    share = scenarios // col_size
    short = lax.dynamic_slice_in_dim(short[0], col * share, share, 0)
    residual = jnp.sqrt(short / (contracts * row_size) + epsilon)
    return (primal_next, dual_next, weight_next, residual)


def solution(mesh):
    in_specs = (
        P("row", "col"),
        P("row", "col"),
        P("col"),
        P("col"),
        P(None, "row"),
        P(None, "col"),
        P(None, "row"),
        P(None, "col"),
        P(None, "row"),
        P(None, "col"),
        P(None, "row"),
        P(),
        P(),
        P(),
    )
    out_specs = (P(None, "col"), P(None, "row"), P(), P("col"))
    return jax.shard_map(shards, mesh=mesh, in_specs=in_specs, out_specs=out_specs, check_vma=False)
```

```python
import jax
import jax.numpy as jnp
from jax import lax
from jax.experimental import pallas as pl
from jax.experimental.pallas import tpu as pltpu
from jax.sharding import PartitionSpec as P

BLOCK = 512
PIECE = 256
ITERS = 3
LANES = 128
MIB = 2**20

epsilon = 1e-06

ROWS_BY_COLS = (((1,), (0,)), ((), ()))
ROWS_BY_ROWS = (((1,), (1,)), ((), ()))
VMEM = pl.BlockSpec(memory_space=pltpu.VMEM)
SMEM = pl.BlockSpec(memory_space=pltpu.SMEM)
HBM = pl.BlockSpec(memory_space=pltpu.HBM)


def f32(*shape):
    return jax.ShapeDtypeStruct(shape, jnp.float32)


def bf16(*shape):
    return jax.ShapeDtypeStruct(shape, jnp.bfloat16)


def launch(body, name, out_shape, args, smem=0, hbm=0, scratch=(), limit=4, flops=10**6, bytes_accessed=10**6):
    outs = jax.tree.map(lambda unused: VMEM, out_shape)
    return pl.pallas_call(
        body,
        name=name,
        out_shape=out_shape,
        in_specs=[SMEM] * smem + [HBM] * hbm + [VMEM] * (len(args) - smem - hbm),
        out_specs=outs,
        scratch_shapes=list(scratch),
        compiler_params=pltpu.CompilerParams(vmem_limit_bytes=limit * MIB),
        cost_estimate=pl.CostEstimate(flops=flops, bytes_accessed=bytes_accessed, transcendentals=0),
    )(*args)


def span(index, size):
    return pl.ds(pl.multiple_of(index * size, size), size)


def column(row):
    n = row.shape[1]
    shape = (n, n)
    diagonal = lax.broadcasted_iota(jnp.int32, shape, 0) == lax.broadcasted_iota(jnp.int32, shape, 1)
    return jnp.sum(jnp.where(diagonal, jnp.broadcast_to(row, shape), 0), axis=1, keepdims=True)


def as_row(col):
    shape = (col.shape[0], LANES)
    diagonal = lax.broadcasted_iota(jnp.int32, shape, 0) == lax.broadcasted_iota(jnp.int32, shape, 1)
    row = jnp.sum(jnp.where(diagonal, jnp.broadcast_to(col, shape), 0.0), axis=0, keepdims=True)
    return jnp.broadcast_to(row, (8, LANES))


def blocks_of(matrix):
    return matrix.shape[0] // BLOCK, matrix.shape[1] // BLOCK


def fetch_blocks(eligible, matrix, held, sems, by_rows):
    block_rows, block_cols = blocks_of(matrix)

    def copy(i, j):
        part = (span(i, BLOCK), span(j, BLOCK))
        return pltpu.make_async_copy(matrix.at[part], held.at[part], sems.at[i, j])

    outer, inner = (block_rows, block_cols) if by_rows else (block_cols, block_rows)

    @pl.loop(0, outer)
    def _(a):
        @pl.loop(0, inner)
        def _(b):
            i, j = (a, b) if by_rows else (b, a)

            @pl.when(eligible(i, j) != 0)
            def _():
                copy(i, j).start()

    return lambda i, j: copy(i, j).wait()


def nothing(i, j):
    return None


def packed_mask(bits, shape):
    word = bits[0, 0]
    return lambda i, j: jnp.bitwise_and(lax.shift_right_logical(word, i * shape[1] + j), 1)


def sum_blocks(eligible, count, multiply, ready, acc, picked):
    found = jnp.int32(0)
    for k in range(count):
        picked[found] = k
        found = found + eligible(k)
    acc[...] = jnp.zeros_like(acc)

    def add(first, number):
        chosen = [picked[first + k] for k in range(number)]
        for k in chosen:
            ready(k)
        terms = [multiply(k) for k in chosen]
        while len(terms) > 1:
            terms = [sum(terms[k : k + 2]) for k in range(0, len(terms), 2)]
        acc[...] += terms[0]

    fours = found // 4

    @pl.loop(0, fours)
    def _(four):
        add(4 * four, 4)

    for rest in (1, 2, 3):
        @pl.when(found - 4 * fours == rest)
        def _():
            add(4 * fours, rest)


def backward_blocks(mask, direct, rounded, held, acc, picked, ready):
    block_rows, block_cols = blocks_of(held)
    scenarios = acc.shape[0]

    @pl.loop(0, block_cols)
    def _(j):
        def multiply(i):
            return lax.dot_general(
                rounded[i], held[span(i, BLOCK), span(j, BLOCK)], ROWS_BY_COLS, preferred_element_type=jnp.float32
            )

        sum_blocks(lambda i: mask(i, j), block_rows, multiply, lambda i: ready(i, j), acc, picked)
        for q in range(BLOCK // PIECE):
            direct[(BLOCK // PIECE) * j + q, :scenarios] = acc[:, q * PIECE : (q + 1) * PIECE]


def first_backward(
    mask, matrix, avg, now, prev, restart, direct, rounded, acc, picked, held, vectors, sems, few
):
    copies = [
        pltpu.make_async_copy(source, vectors.at[k], few.at[k]) for k, source in enumerate((avg, now, prev))
    ]
    for each in copies:
        each.start()
    eligible = lambda i, j: mask[i, j]
    ready = fetch_blocks(eligible, matrix, held, sems, False)
    for each in copies:
        each.wait()
    scenarios = avg.shape[0]
    restarted = column(restart[...]) == 1
    gap = jnp.zeros((scenarios, 1), jnp.float32)
    for i in range(mask.shape[0]):
        cols = slice(i * BLOCK, (i + 1) * BLOCK)
        rounded[i] = jnp.where(restarted, vectors[0, :, cols], vectors[1, :, cols]).astype(jnp.bfloat16)
        gap += jnp.sum(jnp.square(vectors[0, :, cols] - vectors[2, :, cols]), axis=1, keepdims=True)
    backward_blocks(eligible, direct, rounded, held, acc, picked, ready)
    row = as_row(gap)
    for piece in range(direct.shape[0]):
        direct[piece, scenarios:, :LANES] = row
        direct[piece, scenarios:, LANES:] = jnp.zeros_like(row)


def here():
    col = lax.axis_index("col")
    return col // 2, lax.rem(col, 2)


def later_backward(bits, matrix, own, swapped, direct, rounded, acc, picked):
    shape = blocks_of(matrix)
    block_rows = shape[0]
    chip, core = here()
    first = core == 0

    @pl.loop(0, block_rows)
    def _(i):
        slot = lax.rem(i - chip + block_rows, block_rows)
        a = own[slot]
        b = swapped[slot]
        rounded[i, :, :PIECE] = jnp.where(first, a, b).astype(jnp.bfloat16)
        rounded[i, :, PIECE:] = jnp.where(first, b, a).astype(jnp.bfloat16)

    backward_blocks(packed_mask(bits, shape), direct, rounded, matrix, acc, picked, nothing)


def place_pieces(i, value, mine, other, lanes):
    chip, core = here()
    chips = mine.shape[0]
    slot = lax.rem(i - chip + chips, chips)
    low = value[:, :PIECE]
    high = value[:, PIECE:]
    mine[slot, :, lanes] = jnp.where(core == 0, low, high)
    other[slot, :, lanes] = jnp.where(core == 0, high, low)


def forward_blocks(eligible, matrix, mine, other, rounded, acc, picked, ready):
    block_rows, block_cols = blocks_of(matrix)
    scenarios = mine.shape[1]

    @pl.loop(0, block_rows)
    def _(i):
        def multiply(j):
            return lax.dot_general(
                rounded[j], matrix[span(i, BLOCK), span(j, BLOCK)], ROWS_BY_ROWS, preferred_element_type=jnp.float32
            )

        sum_blocks(lambda j: eligible(i, j), block_cols, multiply, lambda j: ready(i, j), acc, picked)
        for group in range(acc.shape[0] // scenarios):
            lanes = slice(group * PIECE, (group + 1) * PIECE)
            place_pieces(i, acc[group * scenarios : (group + 1) * scenarios], mine, other, lanes)


def round_pieces(direct, rounded):
    scenarios = direct.shape[1]
    for piece in range(direct.shape[0]):
        cols = slice(piece % 2 * PIECE, (piece % 2 + 1) * PIECE)
        rounded[piece // 2, :scenarios, cols] = direct[piece].astype(jnp.bfloat16)


def first_forward(matrix, bits, direct, start, mine, other, rounded, acc, picked, held, sems):
    eligible = packed_mask(bits, blocks_of(matrix))
    ready = fetch_blocks(eligible, matrix, held, sems, True)
    scenarios = start.shape[1]
    for j in range(start.shape[0]):
        rounded[j, scenarios:] = start[j]
    round_pieces(direct, rounded)
    forward_blocks(eligible, held, mine, other, rounded, acc, picked, ready)


def later_forward(bits, matrix, direct, mine, other, rounded, acc, picked):
    round_pieces(direct, rounded)
    eligible = packed_mask(bits, blocks_of(matrix))
    forward_blocks(eligible, matrix, mine, other, rounded, acc, picked, nothing)


def prepare(avg, now, prev, restart, gap, rounded):
    restarted = column(restart[...]) == 1
    total = jnp.zeros((avg.shape[0], 1), jnp.float32)
    for j in range(rounded.shape[0]):
        cols = slice(j * BLOCK, (j + 1) * BLOCK)
        rounded[j] = jnp.where(restarted, avg[:, cols], now[:, cols]).astype(jnp.bfloat16)
        total += jnp.sum(jnp.square(avg[:, cols] - prev[:, cols]), axis=1, keepdims=True)
    gap[...] = jnp.broadcast_to(total, gap.shape)


def hold(matrix, near, out):
    out[...] = near[:8, :LANES]


def add_pair(mine, received, *slots):
    for k, slot in enumerate(slots):
        slot[...] = mine[k] + received[k]


def sum_parts(parts):
    total = parts[0]
    for piece in range(1, parts.shape[0]):
        total += parts[piece]
    return total


def step_primal(total, primal, cost, cap, size):
    return jnp.minimum(jnp.maximum(primal - size * (cost[...] - total), 0.0), cap[...])


def spread(value, out):
    for piece in range(out.shape[0]):
        out[piece] = value


def first_primal(
    parts, near, left, across, right, weight, restart, step, primal, cost, cap, out, sizes
):
    total = sum_parts(parts)
    scenarios = primal.shape[0]
    dual_gap = column(total[scenarios : scenarios + 1, :scenarios])
    primal_gap = (near[...] + left[...] + across[...] + right[...])[:, :1]
    old = column(weight[...])
    length = column(step[...])
    ratio = jnp.sqrt((dual_gap + epsilon) / (primal_gap + epsilon))
    weight_next = jnp.where(column(restart[...]) == 1, jnp.sqrt(old * ratio), old)
    primal_size = length / weight_next
    sizes[0] = jnp.broadcast_to(weight_next, sizes.shape[1:])
    sizes[1] = jnp.broadcast_to(primal_size, sizes.shape[1:])
    sizes[2] = jnp.broadcast_to(length * weight_next, sizes.shape[1:])
    spread(step_primal(total[:scenarios], primal[...], cost, cap, primal_size), out)


def later_primal(parts, pieces, cost, cap, sizes, out):
    spread(step_primal(sum_parts(parts), pieces[0], cost, cap, sizes[1, :, :1]), out)


def move_dual(near, left, across, right, image, dual, demand, sizes, image_next, dual_next):
    total = near[...] + left[...] + across[...] + right[...]
    image_new = total[:, :PIECE]
    image_old = total[:, PIECE:] if image is None else image[...]
    moved = demand[...] - 2.0 * image_new + image_old
    dual_next[...] = jnp.maximum(dual[...] + sizes[2, :, :1] * moved, 0.0)
    if image_next is not None:
        image_next[...] = image_new
    return image_new


def later_dual(*refs):
    move_dual(*refs)


def first_dual(held, near, left, across, right, dual, demand, sizes, image_next, dual_next):
    move_dual(near, left, across, right, None, dual, demand, sizes, image_next, dual_next)


def last_dual(near, left, across, right, image, dual, demand, sizes, dual_next, short_out):
    image_new = move_dual(near, left, across, right, image, dual, demand, sizes, None, dual_next)
    short = jnp.sum(jnp.square(jnp.maximum(demand[...] - image_new, 0.0)), axis=1, keepdims=True)
    row = as_row(short)
    for piece in range(short_out.shape[0]):
        short_out[piece] = row


def sum_rows(parts, out):
    out[...] = sum_parts(parts)


def finish(own, swapped, dual_out):
    block_rows = own.shape[0]
    chip, core = here()
    first = core == 0
    for slot in range(block_rows):
        i = lax.rem(chip + slot, block_rows)
        a = own[slot]
        b = swapped[slot]
        dual_out[:, span(2 * i, PIECE)] = jnp.where(first, a, b)
        dual_out[:, span(2 * i + 1, PIECE)] = jnp.where(first, b, a)


def shards(
    matrix,
    band_mask,
    unit_cost,
    capacity,
    demand,
    primal_iter,
    dual_iter,
    primal_avg,
    dual_avg,
    primal_prev,
    dual_prev,
    weight,
    restart,
    plan,
):
    scenarios, segments = primal_iter.shape
    contracts = dual_iter.shape[1]
    block_rows, block_cols = band_mask.shape
    row_size = lax.axis_size("row")
    col_size = lax.axis_size("col")
    chips = col_size // 2
    row = lax.axis_index("row")
    col = lax.axis_index("col")
    blocks = block_rows * block_cols
    bits = jnp.sum(lax.shift_left(band_mask.reshape(blocks), jnp.arange(blocks, dtype=jnp.int32)))
    bits = jnp.broadcast_to(bits, (8, LANES))
    restart_row = restart[None, :]
    weight_row = weight[None, :]
    step_row = (0.4 * jnp.power(0.75, plan.astype(jnp.float32)))[None, :]

    def swap_cores(value):
        return lax.ppermute(value, "col", [(k, k ^ 1) for k in range(col_size)])

    def along_x(value, distance):
        pairs = [(k, (k + 2 * distance) % col_size) for k in range(col_size)]
        return lax.ppermute(value, "col", pairs)

    def exchange(value):
        return lax.all_to_all(value, "row", 0, 0, tiled=True)

    def send(move, slots):
        far = move(slots[2], 2)
        return (slots[0], move(slots[1], 1), far, move(slots[3], 3))

    def spread_round(move, value):
        far = move(value, 2)
        return (value, move(value, 3), far, move(value, 1))

    picked = pltpu.SMEM((block_cols,), jnp.int32)
    block_sems = pltpu.SemaphoreType.DMA((block_rows, block_cols))
    acc = pltpu.VMEM((scenarios, BLOCK), jnp.float32)

    def forward_scratch(count):
        return [
            pltpu.VMEM((block_cols, count, BLOCK), jnp.bfloat16),
            pltpu.VMEM((count, BLOCK), jnp.float32),
            picked,
        ]

    backward_scratch = [pltpu.VMEM((block_rows, scenarios, BLOCK), jnp.bfloat16), acc, picked]
    product = dict(limit=20, flops=8 * 10**8, bytes_accessed=10**7)

    def gather_cols(value):
        own = jnp.stack(spread_round(along_x, value))
        return own, swap_cores(own)

    pieces_shape = f32(row_size, scenarios, PIECE)
    parts = launch(
        first_backward,
        "first_backward",
        f32(row_size, scenarios + 8, PIECE),
        (band_mask, matrix, dual_avg, dual_iter, dual_prev, restart_row),
        smem=1,
        hbm=4,
        scratch=backward_scratch
        + [
            pltpu.VMEM(matrix.shape, jnp.bfloat16),
            pltpu.VMEM((3, scenarios, contracts), jnp.float32),
            block_sems,
            pltpu.SemaphoreType.DMA((3,)),
        ],
        **dict(product, limit=60),
    )
    parts, avg, now, prev = lax.optimization_barrier((parts, primal_avg, primal_iter, primal_prev))
    parts = exchange(parts)
    gap, start = launch(
        prepare,
        "prepare",
        (f32(scenarios, LANES), bf16(block_cols, scenarios, BLOCK)),
        (avg, now, prev, restart_row),
        limit=12,
    )
    gap, bits, start = lax.optimization_barrier((gap, bits, start))
    gap = gap + swap_cores(gap)
    gaps = send(along_x, (gap,) * chips)

    def slice_start(avg, now, first):
        cut = lambda value: lax.dynamic_slice_in_dim(value, first, PIECE, 1)
        return jnp.where(restart[:, None] == 1, cut(avg), cut(now))

    primal = slice_start(primal_avg, primal_iter, row * PIECE)
    cost = lax.dynamic_slice_in_dim(unit_cost, row * PIECE, PIECE, 0)[None, :]
    cap = lax.dynamic_slice_in_dim(capacity, row * PIECE, PIECE, 0)[None, :]
    dual = slice_start(dual_avg, dual_iter, col * PIECE)
    demand_slice = lax.dynamic_slice_in_dim(demand, col * PIECE, PIECE, 1)

    pieces, sizes = launch(
        first_primal,
        "first_primal",
        (pieces_shape, f32(3, scenarios, LANES)),
        (parts, *gaps, weight_row, restart_row, step_row, primal, cost, cap),
        limit=8,
        bytes_accessed=4 * 10**7,
    )
    for iteration in range(ITERS):
        if iteration > 0:
            parts = launch(
                later_backward,
                "later_backward",
                pieces_shape,
                (bits, matrix, own, swapped),
                scratch=backward_scratch,
                **product,
            )
            parts = exchange(parts)
            pieces = launch(
                later_primal, "later_primal", pieces_shape, (parts, pieces, cost, cap, sizes), limit=8
            )
        gathered = exchange(pieces)
        width = 2 * PIECE if iteration == 0 else PIECE
        slots_shape = f32(chips, scenarios, width)
        if iteration == 0:
            mine, other = launch(
                first_forward,
                "first_forward",
                (slots_shape, slots_shape),
                (matrix, bits, gathered, start),
                hbm=1,
                scratch=forward_scratch(2 * scenarios) + [pltpu.VMEM(matrix.shape, jnp.bfloat16), block_sems],
                **dict(product, limit=52),
            )
        else:
            mine, other = launch(
                later_forward,
                "later_forward",
                (slots_shape, slots_shape),
                (bits, matrix, gathered),
                scratch=forward_scratch(scenarios),
                **product,
            )
        received = swap_cores(other)
        if iteration == ITERS - 1:
            primal_next = jnp.transpose(gathered, (1, 0, 2)).reshape(scenarios, segments)
            weight_next = sizes[0, :, 0]
            received, primal_next, weight_next = lax.optimization_barrier((received, primal_next, weight_next))
        slots = launch(add_pair, "add_pair", (f32(scenarios, width),) * chips, (mine, received), limit=8)
        arrived = send(along_x, slots)
        own_value = f32(scenarios, PIECE)
        if iteration == 0:
            taken = launch(hold, "hold", f32(8, LANES), (matrix, slots[0]), limit=20)
            image, dual = launch(
                first_dual,
                "first_dual",
                (own_value, own_value),
                (taken, *arrived, dual, demand_slice, sizes),
            )
        elif iteration < ITERS - 1:
            image, dual = launch(
                later_dual, "later_dual", (own_value, own_value), (*arrived, image, dual, demand_slice, sizes)
            )
        else:
            dual, short = launch(
                last_dual,
                "last_dual",
                (own_value, f32(row_size, 8, LANES)),
                (*arrived, image, dual, demand_slice, sizes),
            )
            short = exchange(short)
        own, swapped = gather_cols(dual)

    dual_next = launch(finish, "finish", f32(scenarios, contracts), (own, swapped))
    short = launch(sum_rows, "sum_rows", f32(8, LANES), (short,))
    short = short + swap_cores(short)
    short = sum(send(along_x, (short,) * chips))
    share = scenarios // col_size
    short = lax.dynamic_slice_in_dim(short[0], col * share, share, 0)
    residual = jnp.sqrt(short / (contracts * row_size) + epsilon)
    return (primal_next, dual_next, weight_next, residual)


def solution(mesh):
    in_specs = (
        P("row", "col"),
        P("row", "col"),
        P("col"),
        P("col"),
        P(None, "row"),
        P(None, "col"),
        P(None, "row"),
        P(None, "col"),
        P(None, "row"),
        P(None, "col"),
        P(None, "row"),
        P(),
        P(),
        P(),
    )
    out_specs = (P(None, "col"), P(None, "row"), P(), P("col"))
    return jax.shard_map(shards, mesh=mesh, in_specs=in_specs, out_specs=out_specs, check_vma=False)
```

```python
import jax
import jax.numpy as jnp
from jax import lax
from jax.experimental import pallas as pl
from jax.experimental.pallas import tpu as pltpu
from jax.sharding import PartitionSpec as P

BLOCK = 512
PIECE = 256
ITERS = 3
LANES = 128
MIB = 2**20

epsilon = 1e-06

ROWS_BY_COLS = (((1,), (0,)), ((), ()))
ROWS_BY_ROWS = (((1,), (1,)), ((), ()))
VMEM = pl.BlockSpec(memory_space=pltpu.VMEM)
SMEM = pl.BlockSpec(memory_space=pltpu.SMEM)
HBM = pl.BlockSpec(memory_space=pltpu.HBM)


def f32(*shape):
    return jax.ShapeDtypeStruct(shape, jnp.float32)


def bf16(*shape):
    return jax.ShapeDtypeStruct(shape, jnp.bfloat16)


def launch(body, name, out_shape, args, smem=0, hbm=0, scratch=(), limit=4, flops=10**6, bytes_accessed=10**6):
    outs = jax.tree.map(lambda unused: VMEM, out_shape)
    return pl.pallas_call(
        body,
        name=name,
        out_shape=out_shape,
        in_specs=[SMEM] * smem + [HBM] * hbm + [VMEM] * (len(args) - smem - hbm),
        out_specs=outs,
        scratch_shapes=list(scratch),
        compiler_params=pltpu.CompilerParams(vmem_limit_bytes=limit * MIB),
        cost_estimate=pl.CostEstimate(flops=flops, bytes_accessed=bytes_accessed, transcendentals=0),
    )(*args)


def span(index, size):
    return pl.ds(pl.multiple_of(index * size, size), size)


def column(row):
    n = row.shape[1]
    shape = (n, n)
    diagonal = lax.broadcasted_iota(jnp.int32, shape, 0) == lax.broadcasted_iota(jnp.int32, shape, 1)
    return jnp.sum(jnp.where(diagonal, jnp.broadcast_to(row, shape), 0), axis=1, keepdims=True)


def as_row(col):
    shape = (col.shape[0], LANES)
    diagonal = lax.broadcasted_iota(jnp.int32, shape, 0) == lax.broadcasted_iota(jnp.int32, shape, 1)
    row = jnp.sum(jnp.where(diagonal, jnp.broadcast_to(col, shape), 0.0), axis=0, keepdims=True)
    return jnp.broadcast_to(row, (8, LANES))


def blocks_of(matrix):
    return matrix.shape[0] // BLOCK, matrix.shape[1] // BLOCK


def fetch_blocks(eligible, matrix, held, sems, by_rows):
    block_rows, block_cols = blocks_of(matrix)

    def copy(i, j):
        part = (span(i, BLOCK), span(j, BLOCK))
        return pltpu.make_async_copy(matrix.at[part], held.at[part], sems.at[i, j])

    outer, inner = (block_rows, block_cols) if by_rows else (block_cols, block_rows)

    @pl.loop(0, outer)
    def _(a):
        @pl.loop(0, inner)
        def _(b):
            i, j = (a, b) if by_rows else (b, a)

            @pl.when(eligible(i, j) != 0)
            def _():
                copy(i, j).start()

    return lambda i, j: copy(i, j).wait()


def nothing(i, j):
    return None


def packed_mask(bits, shape):
    word = bits[0, 0]
    return lambda i, j: jnp.bitwise_and(lax.shift_right_logical(word, i * shape[1] + j), 1)


def sum_blocks(eligible, count, multiply, ready, acc, picked):
    found = jnp.int32(0)
    for k in range(count):
        picked[found] = k
        found = found + eligible(k)
    acc[...] = jnp.zeros_like(acc)

    def add(first, number):
        chosen = [picked[first + k] for k in range(number)]
        for k in chosen:
            ready(k)
        terms = [multiply(k) for k in chosen]
        while len(terms) > 1:
            terms = [sum(terms[k : k + 2]) for k in range(0, len(terms), 2)]
        acc[...] += terms[0]

    fours = found // 4

    @pl.loop(0, fours)
    def _(four):
        add(4 * four, 4)

    @pl.when(found - 4 * fours >= 2)
    def _():
        add(4 * fours, 2)

    @pl.when(lax.rem(found, 2) == 1)
    def _():
        add(found - 1, 1)


def backward_blocks(mask, direct, rounded, held, acc, picked, ready):
    block_rows, block_cols = blocks_of(held)
    scenarios = acc.shape[0]

    @pl.loop(0, block_cols)
    def _(j):
        def multiply(i):
            return lax.dot_general(
                rounded[i], held[span(i, BLOCK), span(j, BLOCK)], ROWS_BY_COLS, preferred_element_type=jnp.float32
            )

        sum_blocks(lambda i: mask(i, j), block_rows, multiply, lambda i: ready(i, j), acc, picked)
        for q in range(BLOCK // PIECE):
            direct[(BLOCK // PIECE) * j + q, :scenarios] = acc[:, q * PIECE : (q + 1) * PIECE]


def first_backward(
    mask, matrix, avg, now, prev, restart, direct, rounded, acc, picked, held, vectors, sems, few
):
    copies = [
        pltpu.make_async_copy(source, vectors.at[k], few.at[k]) for k, source in enumerate((avg, now, prev))
    ]
    for each in copies:
        each.start()
    eligible = lambda i, j: mask[i, j]
    ready = fetch_blocks(eligible, matrix, held, sems, False)
    for each in copies:
        each.wait()
    scenarios = avg.shape[0]
    restarted = column(restart[...]) == 1
    gap = jnp.zeros((scenarios, 1), jnp.float32)
    for i in range(mask.shape[0]):
        cols = slice(i * BLOCK, (i + 1) * BLOCK)
        rounded[i] = jnp.where(restarted, vectors[0, :, cols], vectors[1, :, cols]).astype(jnp.bfloat16)
        gap += jnp.sum(jnp.square(vectors[0, :, cols] - vectors[2, :, cols]), axis=1, keepdims=True)
    backward_blocks(eligible, direct, rounded, held, acc, picked, ready)
    row = as_row(gap)
    for piece in range(direct.shape[0]):
        direct[piece, scenarios:, :LANES] = row
        direct[piece, scenarios:, LANES:] = jnp.zeros_like(row)


def here():
    col = lax.axis_index("col")
    return col // 2, lax.rem(col, 2)


def later_backward(bits, matrix, own, swapped, direct, rounded, acc, picked):
    shape = blocks_of(matrix)
    block_rows = shape[0]
    chip, core = here()
    first = core == 0

    @pl.loop(0, block_rows)
    def _(i):
        slot = lax.rem(i - chip + block_rows, block_rows)
        a = own[slot]
        b = swapped[slot]
        rounded[i, :, :PIECE] = jnp.where(first, a, b).astype(jnp.bfloat16)
        rounded[i, :, PIECE:] = jnp.where(first, b, a).astype(jnp.bfloat16)

    backward_blocks(packed_mask(bits, shape), direct, rounded, matrix, acc, picked, nothing)


def place_pieces(i, value, mine, other, lanes):
    chip, core = here()
    chips = mine.shape[0]
    slot = lax.rem(i - chip + chips, chips)
    low = value[:, :PIECE]
    high = value[:, PIECE:]
    mine[slot, :, lanes] = jnp.where(core == 0, low, high)
    other[slot, :, lanes] = jnp.where(core == 0, high, low)


def forward_blocks(eligible, matrix, mine, other, rounded, acc, picked, ready):
    block_rows, block_cols = blocks_of(matrix)
    scenarios = mine.shape[1]

    @pl.loop(0, block_rows)
    def _(i):
        def multiply(j):
            return lax.dot_general(
                rounded[j], matrix[span(i, BLOCK), span(j, BLOCK)], ROWS_BY_ROWS, preferred_element_type=jnp.float32
            )

        sum_blocks(lambda j: eligible(i, j), block_cols, multiply, lambda j: ready(i, j), acc, picked)
        for group in range(acc.shape[0] // scenarios):
            lanes = slice(group * PIECE, (group + 1) * PIECE)
            place_pieces(i, acc[group * scenarios : (group + 1) * scenarios], mine, other, lanes)


def round_pieces(direct, rounded):
    scenarios = direct.shape[1]
    for piece in range(direct.shape[0]):
        cols = slice(piece % 2 * PIECE, (piece % 2 + 1) * PIECE)
        rounded[piece // 2, :scenarios, cols] = direct[piece].astype(jnp.bfloat16)


def first_forward(matrix, bits, direct, start, mine, other, rounded, acc, picked, held, sems):
    eligible = packed_mask(bits, blocks_of(matrix))
    ready = fetch_blocks(eligible, matrix, held, sems, True)
    scenarios = start.shape[1]
    for j in range(start.shape[0]):
        rounded[j, scenarios:] = start[j]
    round_pieces(direct, rounded)
    forward_blocks(eligible, held, mine, other, rounded, acc, picked, ready)


def later_forward(bits, matrix, direct, mine, other, rounded, acc, picked):
    round_pieces(direct, rounded)
    eligible = packed_mask(bits, blocks_of(matrix))
    forward_blocks(eligible, matrix, mine, other, rounded, acc, picked, nothing)


def prepare(avg, now, prev, restart, gap, rounded):
    restarted = column(restart[...]) == 1
    total = jnp.zeros((avg.shape[0], 1), jnp.float32)
    for j in range(rounded.shape[0]):
        cols = slice(j * BLOCK, (j + 1) * BLOCK)
        rounded[j] = jnp.where(restarted, avg[:, cols], now[:, cols]).astype(jnp.bfloat16)
        total += jnp.sum(jnp.square(avg[:, cols] - prev[:, cols]), axis=1, keepdims=True)
    gap[...] = jnp.broadcast_to(total, gap.shape)


def hold(matrix, near, out):
    out[...] = near[:8, :LANES]


def add_pair(mine, received, *slots):
    for k, slot in enumerate(slots):
        slot[...] = mine[k] + received[k]


def sum_parts(parts):
    total = parts[0]
    for piece in range(1, parts.shape[0]):
        total += parts[piece]
    return total


def step_primal(total, primal, cost, cap, size):
    return jnp.minimum(jnp.maximum(primal - size * (cost[...] - total), 0.0), cap[...])


def spread(value, out):
    for piece in range(out.shape[0]):
        out[piece] = value


def first_primal(
    parts, near, left, across, right, weight, restart, step, primal, cost, cap, out, sizes
):
    total = sum_parts(parts)
    scenarios = primal.shape[0]
    dual_gap = column(total[scenarios : scenarios + 1, :scenarios])
    primal_gap = (near[...] + left[...] + across[...] + right[...])[:, :1]
    old = column(weight[...])
    length = column(step[...])
    ratio = jnp.sqrt((dual_gap + epsilon) / (primal_gap + epsilon))
    weight_next = jnp.where(column(restart[...]) == 1, jnp.sqrt(old * ratio), old)
    primal_size = length / weight_next
    sizes[0] = jnp.broadcast_to(weight_next, sizes.shape[1:])
    sizes[1] = jnp.broadcast_to(primal_size, sizes.shape[1:])
    sizes[2] = jnp.broadcast_to(length * weight_next, sizes.shape[1:])
    spread(step_primal(total[:scenarios], primal[...], cost, cap, primal_size), out)


def later_primal(parts, pieces, cost, cap, sizes, out):
    spread(step_primal(sum_parts(parts), pieces[0], cost, cap, sizes[1, :, :1]), out)


def move_dual(near, left, across, right, image, dual, demand, sizes, image_next, dual_next):
    total = near[...] + left[...] + across[...] + right[...]
    image_new = total[:, :PIECE]
    image_old = total[:, PIECE:] if image is None else image[...]
    moved = demand[...] - 2.0 * image_new + image_old
    dual_next[...] = jnp.maximum(dual[...] + sizes[2, :, :1] * moved, 0.0)
    if image_next is not None:
        image_next[...] = image_new
    return image_new


def later_dual(*refs):
    move_dual(*refs)


def first_dual(held, near, left, across, right, dual, demand, sizes, image_next, dual_next):
    move_dual(near, left, across, right, None, dual, demand, sizes, image_next, dual_next)


def last_dual(near, left, across, right, image, dual, demand, sizes, dual_next, short_out):
    image_new = move_dual(near, left, across, right, image, dual, demand, sizes, None, dual_next)
    short = jnp.sum(jnp.square(jnp.maximum(demand[...] - image_new, 0.0)), axis=1, keepdims=True)
    row = as_row(short)
    for piece in range(short_out.shape[0]):
        short_out[piece] = row


def sum_rows(parts, out):
    out[...] = sum_parts(parts)


def finish(own, swapped, dual_out):
    block_rows = own.shape[0]
    chip, core = here()
    first = core == 0
    for slot in range(block_rows):
        i = lax.rem(chip + slot, block_rows)
        a = own[slot]
        b = swapped[slot]
        dual_out[:, span(2 * i, PIECE)] = jnp.where(first, a, b)
        dual_out[:, span(2 * i + 1, PIECE)] = jnp.where(first, b, a)


def shards(
    matrix,
    band_mask,
    unit_cost,
    capacity,
    demand,
    primal_iter,
    dual_iter,
    primal_avg,
    dual_avg,
    primal_prev,
    dual_prev,
    weight,
    restart,
    plan,
):
    scenarios, segments = primal_iter.shape
    contracts = dual_iter.shape[1]
    block_rows, block_cols = band_mask.shape
    row_size = lax.axis_size("row")
    col_size = lax.axis_size("col")
    chips = col_size // 2
    row = lax.axis_index("row")
    col = lax.axis_index("col")
    blocks = block_rows * block_cols
    bits = jnp.sum(lax.shift_left(band_mask.reshape(blocks), jnp.arange(blocks, dtype=jnp.int32)))
    bits = jnp.broadcast_to(bits, (8, LANES))
    restart_row = restart[None, :]
    weight_row = weight[None, :]
    step_row = (0.4 * jnp.power(0.75, plan.astype(jnp.float32)))[None, :]

    def swap_cores(value):
        return lax.ppermute(value, "col", [(k, k ^ 1) for k in range(col_size)])

    def along_x(value, distance):
        pairs = [(k, (k + 2 * distance) % col_size) for k in range(col_size)]
        return lax.ppermute(value, "col", pairs)

    def exchange(value):
        return lax.all_to_all(value, "row", 0, 0, tiled=True)

    def send(move, slots):
        far = move(slots[2], 2)
        return (slots[0], move(slots[1], 1), far, move(slots[3], 3))

    def spread_round(move, value):
        far = move(value, 2)
        return (value, move(value, 3), far, move(value, 1))

    picked = pltpu.SMEM((block_cols,), jnp.int32)
    block_sems = pltpu.SemaphoreType.DMA((block_rows, block_cols))
    acc = pltpu.VMEM((scenarios, BLOCK), jnp.float32)

    def forward_scratch(count):
        return [
            pltpu.VMEM((block_cols, count, BLOCK), jnp.bfloat16),
            pltpu.VMEM((count, BLOCK), jnp.float32),
            picked,
        ]

    backward_scratch = [pltpu.VMEM((block_rows, scenarios, BLOCK), jnp.bfloat16), acc, picked]
    product = dict(limit=20, flops=8 * 10**8, bytes_accessed=10**7)

    def gather_cols(value):
        own = jnp.stack(spread_round(along_x, value))
        return own, swap_cores(own)

    pieces_shape = f32(row_size, scenarios, PIECE)
    parts = launch(
        first_backward,
        "first_backward",
        f32(row_size, scenarios + 8, PIECE),
        (band_mask, matrix, dual_avg, dual_iter, dual_prev, restart_row),
        smem=1,
        hbm=4,
        scratch=backward_scratch
        + [
            pltpu.VMEM(matrix.shape, jnp.bfloat16),
            pltpu.VMEM((3, scenarios, contracts), jnp.float32),
            block_sems,
            pltpu.SemaphoreType.DMA((3,)),
        ],
        **dict(product, limit=60),
    )
    parts, avg, now, prev = lax.optimization_barrier((parts, primal_avg, primal_iter, primal_prev))
    parts = exchange(parts)
    gap, start = launch(
        prepare,
        "prepare",
        (f32(scenarios, LANES), bf16(block_cols, scenarios, BLOCK)),
        (avg, now, prev, restart_row),
        limit=12,
    )
    gap, bits, start = lax.optimization_barrier((gap, bits, start))
    gap = gap + swap_cores(gap)
    gaps = send(along_x, (gap,) * chips)

    def slice_start(avg, now, first):
        cut = lambda value: lax.dynamic_slice_in_dim(value, first, PIECE, 1)
        return jnp.where(restart[:, None] == 1, cut(avg), cut(now))

    primal = slice_start(primal_avg, primal_iter, row * PIECE)
    cost = lax.dynamic_slice_in_dim(unit_cost, row * PIECE, PIECE, 0)[None, :]
    cap = lax.dynamic_slice_in_dim(capacity, row * PIECE, PIECE, 0)[None, :]
    dual = slice_start(dual_avg, dual_iter, col * PIECE)
    demand_slice = lax.dynamic_slice_in_dim(demand, col * PIECE, PIECE, 1)

    pieces, sizes = launch(
        first_primal,
        "first_primal",
        (pieces_shape, f32(3, scenarios, LANES)),
        (parts, *gaps, weight_row, restart_row, step_row, primal, cost, cap),
        limit=8,
        bytes_accessed=4 * 10**7,
    )
    for iteration in range(ITERS):
        if iteration > 0:
            parts = launch(
                later_backward,
                "later_backward",
                pieces_shape,
                (bits, matrix, own, swapped),
                scratch=backward_scratch,
                **product,
            )
            parts = exchange(parts)
            pieces = launch(
                later_primal, "later_primal", pieces_shape, (parts, pieces, cost, cap, sizes), limit=8
            )
        gathered = exchange(pieces)
        width = 2 * PIECE if iteration == 0 else PIECE
        slots_shape = f32(chips, scenarios, width)
        if iteration == 0:
            mine, other = launch(
                first_forward,
                "first_forward",
                (slots_shape, slots_shape),
                (matrix, bits, gathered, start),
                hbm=1,
                scratch=forward_scratch(2 * scenarios) + [pltpu.VMEM(matrix.shape, jnp.bfloat16), block_sems],
                **dict(product, limit=52),
            )
        else:
            mine, other = launch(
                later_forward,
                "later_forward",
                (slots_shape, slots_shape),
                (bits, matrix, gathered),
                scratch=forward_scratch(scenarios),
                **product,
            )
        received = swap_cores(other)
        if iteration == ITERS - 1:
            primal_next = jnp.transpose(gathered, (1, 0, 2)).reshape(scenarios, segments)
            received, primal_next = lax.optimization_barrier((received, primal_next))
        if iteration == 0:
            weight_next = sizes[0, :, 0]
            received, weight_next = lax.optimization_barrier((received, weight_next))
        slots = launch(add_pair, "add_pair", (f32(scenarios, width),) * chips, (mine, received), limit=8)
        arrived = send(along_x, slots)
        own_value = f32(scenarios, PIECE)
        if iteration == 0:
            taken = launch(hold, "hold", f32(8, LANES), (matrix, slots[0]), limit=20)
            image, dual = launch(
                first_dual,
                "first_dual",
                (own_value, own_value),
                (taken, *arrived, dual, demand_slice, sizes),
            )
        elif iteration < ITERS - 1:
            image, dual = launch(
                later_dual, "later_dual", (own_value, own_value), (*arrived, image, dual, demand_slice, sizes)
            )
        else:
            dual, short = launch(
                last_dual,
                "last_dual",
                (own_value, f32(row_size, 8, LANES)),
                (*arrived, image, dual, demand_slice, sizes),
            )
            short = exchange(short)
        own, swapped = gather_cols(dual)

    dual_next = launch(finish, "finish", f32(scenarios, contracts), (own, swapped))
    short = launch(sum_rows, "sum_rows", f32(8, LANES), (short,))
    short = short + swap_cores(short)
    short = sum(send(along_x, (short,) * chips))
    share = scenarios // col_size
    short = lax.dynamic_slice_in_dim(short[0], col * share, share, 0)
    residual = jnp.sqrt(short / (contracts * row_size) + epsilon)
    return (primal_next, dual_next, weight_next, residual)


def solution(mesh):
    in_specs = (
        P("row", "col"),
        P("row", "col"),
        P("col"),
        P("col"),
        P(None, "row"),
        P(None, "col"),
        P(None, "row"),
        P(None, "col"),
        P(None, "row"),
        P(None, "col"),
        P(None, "row"),
        P(),
        P(),
        P(),
    )
    out_specs = (P(None, "col"), P(None, "row"), P(), P("col"))
    return jax.shard_map(shards, mesh=mesh, in_specs=in_specs, out_specs=out_specs, check_vma=False)
```
